32 devices in a mesh: rows: 16 (over z, y, core), seq: 2 (over x).
Axes of the slice: x: 2, y: 2, z: 4, core: 2. Of those that a mesh axis runs over, the one named last changes fastest.
Arguments:
- inputs: bfloat16 [16, 1024, 768], P('rows', 'seq'), may hold values from -6 to 6
- seg_start: int32 [16, 1024], P('rows', 'seq'), may hold values from -1 to 576, as said below
- w_query: bfloat16 [2, 768, 768], P(None, 'rows'), may hold values from -0.21875 to 0.21875
- w_key: bfloat16 [2, 768, 768], P(None, 'rows'), may hold values from -0.21875 to 0.21875
- w_value: bfloat16 [2, 768, 768], P(None, 'rows'), may hold values from -0.21875 to 0.21875
- w_out: bfloat16 [2, 768, 768], P(None, 'rows'), may hold values from -1.75 to 1.75
- w_gate: bfloat16 [2, 768, 2048], P(None, 'rows'), may hold values from -0.21875 to 0.21875
- w_up: bfloat16 [2, 768, 2048], P(None, 'rows'), may hold values from -0.21875 to 0.21875
- w_down: bfloat16 [2, 2048, 768], P(None, 'rows'), may hold values from -0.125 to 0.125
- norm_attn: bfloat16 [2, 768], P(None, 'rows'), may hold values from 0.5 to 1.5
- norm_mlp: bfloat16 [2, 768], P(None, 'rows'), may hold values from 0.5 to 1.5
- cotangent: bfloat16 [16, 1024, 768], P('rows', 'seq'), may hold values from -6 to 6
Outputs:
- output: float32 [16, 1024, 768], P('rows', 'seq')
- grad_input: float32 [16, 1024, 768], P('rows', 'seq')
- grad_query: float32 [2, 768, 768], P(None, 'rows')
- grad_key: float32 [2, 768, 768], P(None, 'rows')
- grad_value: float32 [2, 768, 768], P(None, 'rows')
- grad_out: float32 [2, 768, 768], P(None, 'rows')
- grad_gate: float32 [2, 768, 2048], P(None, 'rows')
- grad_up: float32 [2, 768, 2048], P(None, 'rows')
- grad_down: float32 [2, 2048, 768], P(None, 'rows')
- grad_norm_attn: float32 [2, 768], P(None, 'rows')
- grad_norm_mlp: float32 [2, 768], P(None, 'rows')
The draws below stay inside these ranges and needn't reach their ends.
Inputs may be any that keep to these rules, and one draw needn't show every extreme that they name: `seg_start`: each row holds whole images of 576 or 256 tokens laid end to end from position 0, none beginning after position 576; every token of an image carries the image's first position; the rest of the row, one position or more, is padding and carries -1.
All inputs are finite; a program needn't handle non-finite values.
Results may differ from the reference program's by a relative error of at most 0.025.
Values may be sent and summed in bfloat16 or wider, within the bound.
No kernel may reach another device: no remote copies, remote signals or barrier semaphores. Data moves between devices by JAX's collectives and lax.ppermute only.
A program may use at most 448 MiB of HBM per device.

```python
import jax
import jax.numpy as jnp
from jax import lax

D = 768
HEADS = 12
HEAD_DIM = 64
FF = 2048
LAYERS = 2
LEN = 1024
IMG_BIG = 576
IMG_SMALL = 256
ROWS_DEV = 1
ROWS = 16
N_ROWS = 16


def draw_seg_start(key, part):
    count = LEN // IMG_SMALL + 1
    picks = jax.random.randint(key, (ROWS, count), 0, 2)
    picks = picks.at[0, 0].set(1).at[0, 1].set(0)
    lengths = jnp.where(picks == 1, IMG_BIG, IMG_SMALL).astype(jnp.int32)
    ends = jnp.cumsum(lengths, axis=1)
    begins = ends - lengths
    fitting = (ends <= LEN - 1) & (begins <= IMG_BIG)
    index = jnp.arange(LEN, dtype=jnp.int32)
    inside = (index[None, None, :] >= begins[:, :, None]) & (index[None, None, :] < ends[:, :, None]) & fitting[:, :, None]
    first_pos = jnp.sum(jnp.where(inside, begins[:, :, None], 0), axis=1)
    covered = jnp.any(inside, axis=1)
    return jnp.where(covered, first_pos, -1).astype(jnp.int32)


def raised(values, key, source, target, parts, factor):
    def block_of(axis_at):
        return (jnp.arange(values.shape[axis_at]) // (values.shape[axis_at] // parts)).reshape((-1,) + (1,) * (values.ndim - 1 - axis_at))

    one_side = jax.random.permutation(key, parts)[block_of(target)]
    far = (block_of(target) + parts // 2) % parts
    return jnp.where((block_of(source) == one_side) | (block_of(source) == far), factor * values, values)


def block_levels(key, dims, pieces, smallest, top_value):
    def one(axis_at, blocks):
        heights = jax.random.uniform(jax.random.fold_in(jax.random.fold_in(key, 6), axis_at), (blocks,), jnp.float32, smallest / len(pieces), top_value / len(pieces))
        return jnp.repeat(jnp.exp(heights), dims[axis_at] // blocks).reshape((-1,) + (1,) * (len(dims) - axis_at - 1))

    loudness = one(*pieces[0])
    for cut in pieces[1:]:
        loudness = loudness * one(*cut)
    return loudness


def scatter_about(key, extent, scale, limit, cuts=(), held_as=jnp.bfloat16):
    values = scale * jax.random.normal(key, extent, jnp.float32)
    if cuts:
        values = values * block_levels(key, extent, cuts, -0.22, 0.18)
    return jnp.clip(values, -limit, limit).astype(held_as)


def noise_with(rng, extent, width, bound, cuts, heavy, held_as=jnp.bfloat16):
    array = width * jax.random.normal(rng, extent, jnp.float32)
    if cuts:
        array = array * block_levels(rng, extent, cuts, -0.22, 0.18)
    return jnp.clip(raised(array, jax.random.fold_in(rng, 3), *heavy), -bound, bound).astype(held_as)


def setup_inputs(seed: int = 0) -> dict:
    streams_of = jax.random.split(jax.random.key(seed), 13)
    return {
        "inputs": noise_with(streams_of[0], (ROWS, LEN, D), 1.0, 6.0, ((0, 16), (1, 2)), (0, 2, 16, 2.0)),
        "seg_start": draw_seg_start(jax.random.fold_in(streams_of[12], 71), 0),
        "w_query": scatter_about(streams_of[2], (LAYERS, D, D), D ** -0.5, 0.21875, ((1, 16),)),
        "w_key": scatter_about(streams_of[3], (LAYERS, D, D), D ** -0.5, 0.21875, ((1, 16),)),
        "w_value": scatter_about(streams_of[4], (LAYERS, D, D), D ** -0.5, 0.21875, ((1, 16),)),
        "w_out": scatter_about(streams_of[5], (LAYERS, D, D), (D // 64) ** -0.5, 1.75, ((1, 16),)),
        "w_gate": scatter_about(streams_of[6], (LAYERS, D, FF), D ** -0.5, 0.21875, ((1, 16),)),
        "w_up": scatter_about(streams_of[7], (LAYERS, D, FF), D ** -0.5, 0.21875, ((1, 16),)),
        "w_down": scatter_about(streams_of[8], (LAYERS, FF, D), FF ** -0.5, 0.125, ((1, 16),)),
        "norm_attn": jnp.clip(1.0 + 0.1 * jax.random.normal(streams_of[9], (LAYERS, D), jnp.float32), 0.5, 1.5).astype(jnp.bfloat16),
        "norm_mlp": jnp.clip(1.0 + 0.1 * jax.random.normal(streams_of[10], (LAYERS, D), jnp.float32), 0.5, 1.5).astype(jnp.bfloat16),
        "cotangent": scatter_about(streams_of[11], (ROWS, LEN, D), 1.0, 6.0, ((0, 16), (1, 2))),
    }


EPS = 1e-05
NEG_BIG = -1e+30
THETA = 10000.0
HIGH = lax.Precision.HIGHEST

@jax.custom_vjp
def low(v):
    return lax.optimization_barrier(v.astype(jnp.bfloat16)).astype(jnp.float32)

@jax.custom_vjp
def low_back(v):
    return v

def low_keep(v):
    return (low(v), None)

def low_pass(kept, grad):
    return (grad,)

def back_keep(v):
    return (v, None)

def back_low(kept, grad):
    return (low(grad),)
low.defvjp(low_keep, low_pass)
low_back.defvjp(back_keep, back_low)

def rope_tables(positions):
    half = HEAD_DIM // 2
    inverse = THETA ** (-jnp.arange(half, dtype=jnp.float32) * 2.0 / HEAD_DIM)
    angles = positions.astype(jnp.float32)[..., None] * inverse
    return (jnp.cos(angles)[..., None, :], jnp.sin(angles)[..., None, :])

def rotate(tensor, cosine, sine):
    half = tensor.shape[-1] // 2
    first = tensor[..., :half]
    second = tensor[..., half:]
    return jnp.concatenate([first * cosine - second * sine, second * cosine + first * sine], -1)

def rms_gain(hidden, gain):
    return hidden * lax.rsqrt(lax.optimization_barrier(jnp.mean(hidden * hidden, -1, keepdims=True)) + EPS) * gain

def project(left, matrix):
    return jnp.einsum('gtd,df->gtf', left, matrix, precision=HIGH)

def attend_row(operands):
    queries, key_rows, values, starts = operands
    index = jnp.arange(LEN, dtype=jnp.int32)
    same = (starts[:, None] == starts[None, :]) & (starts[:, None] >= 0) & (index[None, :] <= index[:, None])
    allowed = same | (index[None, :] == index[:, None])
    scores = low_back(jnp.einsum('qhd,khd->hqk', queries, key_rows, precision=HIGH) * HEAD_DIM ** (-0.5))
    scores = jnp.where(allowed[None], scores, NEG_BIG)
    highest = lax.optimization_barrier(jnp.max(scores, -1, keepdims=True))
    expd = jnp.exp(scores - highest)
    probs = expd / lax.optimization_barrier(jnp.sum(expd, -1, keepdims=True))
    return jnp.einsum('hqk,khd->qhd', low(probs), values, precision=HIGH)

def layer(hidden_in, starts, weights):
    w_q, w_k, w_v, w_o, w_g, w_u, w_d, gain_attn, gain_mlp = weights
    groups = hidden_in.shape[0]
    index = jnp.arange(LEN, dtype=jnp.int32)
    positions = jnp.where(starts >= 0, index[None, :] - starts, 0)
    cosine, sine = rope_tables(positions)
    hidden = low(rms_gain(hidden_in, gain_attn))
    q_pre = low_back(project(hidden, w_q)).reshape(groups, LEN, HEADS, HEAD_DIM)
    k_pre = low_back(project(hidden, w_k)).reshape(groups, LEN, HEADS, HEAD_DIM)
    queries = low(rotate(q_pre, cosine, sine))
    key_rows = low(rotate(k_pre, cosine, sine))
    values = low(low_back(project(hidden, w_v))).reshape(groups, LEN, HEADS, HEAD_DIM)
    mixed = lax.map(jax.checkpoint(attend_row), (queries, key_rows, values, starts))
    attended = low(low_back(mixed.reshape(groups, LEN, D)))
    x_mid = hidden_in + low_back(project(attended, w_o))
    hidden2 = low(rms_gain(x_mid, gain_mlp))
    gate = low_back(project(hidden2, w_g))
    up_val = low_back(project(hidden2, w_u))
    act = low(gate * jax.nn.sigmoid(gate) * up_val)
    return x_mid + low_back(project(act, w_d))

def model(params, hidden_in, starts):
    for layer_idx in range(LAYERS):
        weights = tuple((param[layer_idx] for param in params))
        hidden_in = layer(hidden_in, starts, weights)
    return hidden_in

def reference(inputs, seg_start, w_query, w_key, w_value, w_out, w_gate, w_up, w_down, norm_attn, norm_mlp, cotangent):
    params = tuple((arr.astype(jnp.float32) for arr in (w_query, w_key, w_value, w_out, w_gate, w_up, w_down, norm_attn, norm_mlp)))
    grouped_in = inputs.reshape(N_ROWS, ROWS_DEV, LEN, D)
    grouped_st = seg_start.reshape(N_ROWS, ROWS_DEV, LEN)
    grouped_ct = cotangent.reshape(N_ROWS, ROWS_DEV, LEN, D)

    def group_step(totals, item):
        block_in, block_st, block_ct = item

        def forward(param_set, hidden_in):
            return model(param_set, hidden_in, block_st)
        result, pull = jax.vjp(forward, params, block_in.astype(jnp.float32))
        grad_params, grad_in = pull(block_ct.astype(jnp.float32))
        totals = tuple((acc + grd for acc, grd in zip(totals, grad_params)))
        return (totals, (result, grad_in))
    zeros = tuple((jnp.zeros(param.shape, jnp.float32) for param in params))
    totals, (results, grads_in) = lax.scan(group_step, zeros, (grouped_in, grouped_st, grouped_ct))
    output = results.reshape(ROWS, LEN, D)
    grad_input = grads_in.reshape(ROWS, LEN, D)
    return (output, grad_input, totals[0], totals[1], totals[2], totals[3], totals[4], totals[5], totals[6], totals[7], totals[8])
```

```python
import functools

import jax
import jax.numpy as jnp
from jax import lax
from jax.experimental import pallas as pl
from jax.experimental.pallas import tpu as pltpu
from jax.sharding import PartitionSpec as P

HEADS = 12
HEAD_DIM = 64
LAYERS = 2
EPS = 1e-05
NEG_BIG = -1e30
THETA = 10000.0
F32 = jnp.float32
BF16 = jnp.bfloat16
BOTH = ("rows", "seq")
SMEM = pl.BlockSpec(memory_space=pltpu.SMEM)
VMEM = pl.BlockSpec(memory_space=pltpu.VMEM)
ANY = pl.BlockSpec(memory_space=pl.ANY)
VMEM_BYTES = 56 * 1024 * 1024
Q_TILE = 128
K_TILE = 256


def dot(left, right):
    return jnp.dot(left, right, preferred_element_type=F32)


def dot_nt(left, right):
    return lax.dot_general(left, right, (((1,), (1,)), ((), ())), preferred_element_type=F32)


def swap_halves(block):
    lane = lax.broadcasted_iota(jnp.int32, block.shape, 1)
    return jnp.where(lane % 64 < 32, pltpu.roll(block, 96, 1), pltpu.roll(block, 32, 1))


def start_weights(order, refs, held, sem):
    rows = refs[0].shape[0]
    for index, ref in enumerate(refs):
        at = pl.multiple_of(order[index] * rows, 16)
        pltpu.make_async_copy(ref, held.at[pl.ds(at, rows), :], sem).start()


def wait_whole(held, sem):
    pltpu.make_async_copy(held, held, sem).wait()


def send_out(order, whole, refs, sem):
    index = 0
    for ref in refs:
        for part in range(ref.shape[0]):
            rows = ref.shape[1]
            at = pl.multiple_of(order[index] * rows, 16)
            pltpu.make_async_copy(whole.at[pl.ds(at, rows), :], ref.at[part], sem).start()
            index += 1


def call(kernel, name, out_shape, in_specs, out_specs, scratch, args, flops, nbytes):
    return pl.pallas_call(
        kernel,
        name=name,
        out_shape=out_shape,
        in_specs=in_specs,
        out_specs=out_specs,
        scratch_shapes=scratch,
        compiler_params=pltpu.CompilerParams(vmem_limit_bytes=VMEM_BYTES),
        cost_estimate=pl.CostEstimate(flops=flops, bytes_accessed=nbytes, transcendentals=0),
    )(*args)


def row_tile(tokens):
    return min(256, tokens)


def pre_kernel(n_w, order, x_ref, cos_ref, sin_ref, *refs):
    w_refs = refs[:n_w]
    q_ref, kv_ref, gains_ref, w_s, hid_s, sem = refs[n_w:]
    tokens, width = x_ref.shape
    start_weights(order, w_refs, w_s, sem)
    wait_whole(w_s, sem)
    gains_ref[...] = w_s[:, 3 * width : 3 * width + 128].astype(F32).T[:8]
    gain = gains_ref[0:1, :]
    tile = row_tile(tokens)

    def body(step, carry):
        at = pl.ds(pl.multiple_of(step * tile, tile), tile)
        x = x_ref[at, :].astype(F32)
        factor = lax.rsqrt(jnp.mean(x * x, -1, keepdims=True) + EPS)
        hidden = (x * factor * gain).astype(BF16)
        cosine, sine = cos_ref[at, :], sin_ref[at, :]
        for col in range(0, 3 * width, 256):
            part = dot(hidden, w_s[:, col : col + 256])
            if col < 2 * width:
                halves = []
                for lane in (0, 128):
                    block = part[:, lane : lane + 128]
                    halves.append(block * cosine + swap_halves(block) * sine)
                part = jnp.concatenate(halves, 1)
            if col < width:
                q_ref[at, col : col + 256] = (part * HEAD_DIM**-0.5).astype(BF16)
            else:
                kv_ref[at, col - width : col - width + 256] = part.astype(BF16)
        return carry

    lax.fori_loop(0, tokens // tile, body, 0)


def pre(order, x, cosine, sine, weights):
    tokens, width = x.shape
    cols = weights[0].shape[1]
    return call(
        functools.partial(pre_kernel, len(weights)),
        "pre",
        (
            jax.ShapeDtypeStruct((tokens, width), BF16),
            jax.ShapeDtypeStruct((tokens, 2 * width), BF16),
            jax.ShapeDtypeStruct((8, width), F32),
        ),
        [SMEM, VMEM, VMEM, VMEM] + [ANY] * len(weights),
        (VMEM, VMEM, VMEM),
        [
            pltpu.VMEM((width, cols), BF16),
            pltpu.VMEM((tokens, width), BF16),
            pltpu.SemaphoreType.DMA,
        ],
        (order, x, cosine, sine, *weights),
        2 * tokens * width * 3 * width,
        width * cols * 2 + tokens * width * 10,
    )


def load_bands(bands, kv_refs, kv_s, sem):
    tokens = kv_refs[0].shape[0]
    for index, ref in enumerate(kv_refs):
        at = pl.multiple_of(bands[index + 1] * tokens, tokens)
        pltpu.make_async_copy(ref, kv_s.at[pl.ds(at, tokens), :], sem).start()


def bias_tile(mark_col, mark_row, k_at, q_at, k_tile, q_tile):
    key = k_at + lax.broadcasted_iota(jnp.int32, (k_tile, q_tile), 0)
    query = q_at + lax.broadcasted_iota(jnp.int32, (k_tile, q_tile), 1)
    return jnp.where((mark_col == mark_row) & (key <= query), 0.0, NEG_BIG)


def head_pair(block):
    lane = lax.broadcasted_iota(jnp.int32, block.shape, 1)
    zero = jnp.zeros_like(block)
    return jnp.concatenate(
        [jnp.where(lane < 64, block, zero), jnp.where(lane >= 64, block, zero)], 0
    )


def transpose_into(dest, source, first, columns, rows):
    for col in range(0, columns, 128):
        for row in range(0, rows, 128):
            block = source[row : row + 128, first + col : first + col + 128]
            dest[col : col + 128, row : row + 128] = block.astype(F32).T.astype(BF16)


def attend_kernel(n_kv, low, bands, q_ref, row_ref, col_ref, *refs):
    kv_refs = refs[:n_kv]
    out_ref, lse_ref, kv_s, vt_s, acc_s, max_s, sum_s, sem = refs[n_kv:]
    tokens, width = q_ref.shape
    total = kv_s.shape[0]
    load_bands(bands, kv_refs, kv_s, sem)
    wait_whole(kv_s, sem)
    transpose_into(vt_s, kv_s, width, width, total)
    first = bands[0] * tokens
    lse_ref[...] = jnp.zeros_like(lse_ref)

    def q_step(q_index, carry):
        q_at = pl.multiple_of(q_index * Q_TILE, Q_TILE)
        max_s[...] = jnp.full_like(max_s, NEG_BIG)
        sum_s[...] = jnp.zeros_like(sum_s)
        acc_s[...] = jnp.zeros_like(acc_s)
        mark_row = row_ref[0:1, pl.ds(q_at, Q_TILE)]

        def k_step(k_index, inner):
            k_at = pl.multiple_of(k_index * K_TILE, K_TILE)
            bias = bias_tile(
                col_ref[pl.ds(k_at, K_TILE), :], mark_row, k_at, first + q_at, K_TILE, Q_TILE
            )
            bias = jnp.concatenate([bias, bias], 1)
            for pair in range(HEADS // 2):
                lanes = slice(128 * pair, 128 * pair + 128)
                queries = head_pair(q_ref[pl.ds(q_at, Q_TILE), lanes])
                scores = dot_nt(kv_s[pl.ds(k_at, K_TILE), lanes], queries) + bias
                before = max_s[pair : pair + 1, :]
                highest = jnp.maximum(before, jnp.max(scores, 0, keepdims=True))
                shrink = jnp.exp(before - highest)
                expd = jnp.exp(scores - highest)
                max_s[pair : pair + 1, :] = highest
                sum_s[pair : pair + 1, :] = sum_s[pair : pair + 1, :] * shrink + jnp.sum(
                    expd, 0, keepdims=True
                )
                low_p = expd.astype(BF16)
                for side in (0, 1):
                    heads = slice(128 * pair + 64 * side, 128 * pair + 64 * side + 64)
                    part = slice(Q_TILE * side, Q_TILE * side + Q_TILE)
                    mixed = dot(vt_s[heads, pl.ds(k_at, K_TILE)], low_p[:, part])
                    acc_s[heads, :] = acc_s[heads, :] * shrink[:, part] + mixed
            return inner

        high = (first + q_at + Q_TILE - 1) // K_TILE + 1
        lax.fori_loop(low[q_index], high, k_step, 0)
        for pair in range(HEADS // 2):
            lanes = slice(128 * pair, 128 * pair + 128)
            scale = 1.0 / sum_s[pair : pair + 1, :]
            lse = max_s[pair : pair + 1, :] + jnp.log(sum_s[pair : pair + 1, :])
            both = []
            for side in (0, 1):
                heads = slice(128 * pair + 64 * side, 128 * pair + 64 * side + 64)
                part = slice(Q_TILE * side, Q_TILE * side + Q_TILE)
                both.append(acc_s[heads, :] * scale[:, part])
                row = 2 * pair + side
                lse_ref[row : row + 1, pl.ds(q_at, Q_TILE)] = lse[:, part]
            out_ref[pl.ds(q_at, Q_TILE), lanes] = jnp.concatenate(both, 0).T.astype(BF16)
        return carry

    lax.fori_loop(0, tokens // Q_TILE, q_step, 0)


def attend(low, bands, queries, mark_row, mark_col, kv_list, total):
    tokens, width = queries.shape
    return call(
        functools.partial(attend_kernel, len(kv_list)),
        "attend",
        (
            jax.ShapeDtypeStruct((tokens, width), BF16),
            jax.ShapeDtypeStruct((16, tokens), F32),
        ),
        [SMEM, SMEM, VMEM, VMEM, VMEM] + [ANY] * len(kv_list),
        (VMEM, VMEM),
        [
            pltpu.VMEM((total, 2 * width), BF16),
            pltpu.VMEM((width, total), BF16),
            pltpu.VMEM((width, Q_TILE), F32),
            pltpu.VMEM((8, 2 * Q_TILE), F32),
            pltpu.VMEM((8, 2 * Q_TILE), F32),
            pltpu.SemaphoreType.DMA,
        ],
        (low, bands, queries, mark_row, mark_col, *kv_list),
        8 * tokens * total * width,
        total * width * 4 + tokens * width * 4,
    )


def post_kernel(n_w, order, x_ref, att_ref, gains_ref, *refs):
    a_refs, d_refs = refs[:n_w], refs[n_w : 2 * n_w]
    out_ref, mid_ref, gu_ref, a_s, d_s, act_s, sem_a, sem_d = refs[2 * n_w :]
    tokens, width = x_ref.shape
    ff = d_s.shape[0]
    start_weights(order, a_refs, a_s, sem_a)
    start_weights(order, d_refs, d_s, sem_d)
    wait_whole(a_s, sem_a)
    wait_whole(d_s, sem_d)
    gain = gains_ref[1:2, :]
    tile = row_tile(tokens)

    def body(step, carry):
        at = pl.ds(pl.multiple_of(step * tile, tile), tile)
        mid = x_ref[at, :].astype(F32) + dot(att_ref[at, :], a_s[:, :width])
        mid_ref[at, :] = mid
        factor = lax.rsqrt(jnp.mean(mid * mid, -1, keepdims=True) + EPS)
        hidden = (mid * factor * gain).astype(BF16)
        for col in range(0, ff, 256):
            gate = dot(hidden, a_s[:, width + col : width + col + 256])
            up = dot(hidden, a_s[:, width + ff + col : width + ff + col + 256])
            gu_ref[at, col : col + 256] = gate.astype(BF16)
            gu_ref[at, ff + col : ff + col + 256] = up.astype(BF16)
            act_s[:, col : col + 256] = (gate * jax.nn.sigmoid(gate) * up).astype(BF16)
        out_ref[at, :] = mid + dot(act_s[...], d_s[...])
        return carry

    lax.fori_loop(0, tokens // tile, body, 0)


def post(order, x, attended, gains, w_a, w_d):
    tokens, width = x.shape
    cols = w_a[0].shape[1]
    ff = (cols - width) // 2
    return call(
        functools.partial(post_kernel, len(w_a)),
        "post",
        (
            jax.ShapeDtypeStruct((tokens, width), F32),
            jax.ShapeDtypeStruct((tokens, width), F32),
            jax.ShapeDtypeStruct((tokens, 2 * ff), BF16),
        ),
        [SMEM, VMEM, VMEM, VMEM] + [ANY] * (2 * len(w_a)),
        (VMEM, VMEM, VMEM),
        [
            pltpu.VMEM((width, cols), BF16),
            pltpu.VMEM((ff, width), BF16),
            pltpu.VMEM((row_tile(tokens), ff), BF16),
            pltpu.SemaphoreType.DMA,
            pltpu.SemaphoreType.DMA,
        ],
        (order, x, attended, gains, *w_a, *w_d),
        2 * tokens * width * (cols + ff),
        (width * cols + ff * width) * 2 + tokens * width * 14 + tokens * ff * 4,
    )


def mlp_back_kernel(n_w, n_g, order, order_g, flow_ref, mid_ref, gu_ref, att_ref, gains_ref, *refs):
    a_refs, d_refs = refs[:n_w], refs[n_w : 2 * n_w]
    refs = refs[2 * n_w :]
    dmid_ref, datt_ref, ggain_ref = refs[:3]
    ga_refs, gd_refs = refs[3 : 3 + n_g], refs[3 + n_g : 3 + 2 * n_g]
    a_s, d_s, actt_s, db_s, dgu_s, hidt_s, attt_s, dattn_s, ga_s, gd_s, sem_a, sem_d = refs[
        3 + 2 * n_g :
    ]
    tokens, width = mid_ref.shape
    ff = d_s.shape[0]
    start_weights(order, d_refs, d_s, sem_d)
    start_weights(order, a_refs, a_s, sem_a)
    gain = gains_ref[1:2, :]
    tile = row_tile(tokens)
    wait_whole(d_s, sem_d)
    wait_whole(a_s, sem_a)
    ggain = jnp.zeros((1, width), F32)
    for start in range(0, tokens, tile):
        at = slice(start, start + tile)
        low_flow = flow_ref[at, :].astype(BF16)
        db_s[at, :] = low_flow

        def columns(step, carry, at=at, low_flow=low_flow):
            col = pl.multiple_of(step * 256, 256)
            d_act = dot_nt(low_flow, d_s[pl.ds(col, 256), :])
            gate = gu_ref[at, pl.ds(col, 256)].astype(F32)
            up = gu_ref[at, pl.ds(ff + col, 256)].astype(F32)
            sigma = jax.nn.sigmoid(gate)
            silu = gate * sigma
            actt_s[pl.ds(col, 256), at] = (silu * up).T.astype(BF16)
            dgu_s[at, pl.ds(col, 256)] = (
                d_act * up * (sigma * (1.0 + gate * (1.0 - sigma)))
            ).astype(BF16)
            dgu_s[at, pl.ds(ff + col, 256)] = (d_act * silu).astype(BF16)
            return carry

        lax.fori_loop(0, ff // 256, columns, 0)
        mid = mid_ref[at, :]
        factor = lax.rsqrt(jnp.mean(mid * mid, -1, keepdims=True) + EPS)
        normed = mid * factor
        hidt_s[:, at] = (normed * gain).T.astype(BF16)
        attt_s[:, at] = att_ref[at, :].astype(F32).T.astype(BF16)
        d_hid = dot_nt(dgu_s[at, :], a_s[:, width:])
        ggain = ggain + jnp.sum(d_hid * normed, 0, keepdims=True)
        shaped = d_hid * gain
        d_mid = flow_ref[at, :].astype(F32) + factor * (
            shaped - normed * jnp.mean(shaped * normed, -1, keepdims=True)
        )
        dmid_ref[at, :] = d_mid
        d_attn = d_mid.astype(BF16)
        dattn_s[at, :] = d_attn
        datt_ref[at, :] = dot_nt(d_attn, a_s[:, :width]).astype(BF16)
    ggain_ref[...] = jnp.broadcast_to(ggain, ggain_ref.shape)

    def down_rows(step, carry):
        at = pl.ds(pl.multiple_of(step * 256, 256), 256)
        gd_s[at, :] = dot(actt_s[at, :], db_s[...]).astype(BF16)
        return carry

    lax.fori_loop(0, ff // 256, down_rows, 0)
    send_out(order_g, gd_s, gd_refs, sem_d)
    ga_s[:, :width] = dot(attt_s[...], dattn_s[...]).astype(BF16)

    def gu_columns(step, carry):
        col = pl.multiple_of(step * 256, 256)
        ga_s[:, pl.ds(width + col, 256)] = dot(hidt_s[...], dgu_s[:, pl.ds(col, 256)]).astype(BF16)
        return carry

    lax.fori_loop(0, 2 * ff // 256, gu_columns, 0)
    send_out(order_g, ga_s, ga_refs, sem_a)
    wait_whole(gd_s, sem_d)
    wait_whole(ga_s, sem_a)


def mlp_back(order, order_g, parts, flow, mid, gu, attended, gains, w_a, w_d):
    tokens, width = mid.shape
    cols = w_a[0].shape[1]
    ff = (cols - width) // 2
    n_g, per, pieces = parts
    ga = jax.ShapeDtypeStruct((per, width // pieces, cols), BF16)
    gd = jax.ShapeDtypeStruct((per, ff // pieces, width), BF16)
    return call(
        functools.partial(mlp_back_kernel, len(w_a), n_g),
        "mlp_back",
        (
            jax.ShapeDtypeStruct((tokens, width), F32),
            jax.ShapeDtypeStruct((tokens, width), BF16),
            jax.ShapeDtypeStruct((8, width), F32),
            *([ga] * n_g),
            *([gd] * n_g),
        ),
        [SMEM, SMEM] + [VMEM] * 5 + [ANY] * (2 * len(w_a)),
        (VMEM, VMEM, VMEM, *([ANY] * (2 * n_g))),
        [
            pltpu.VMEM((width, cols), BF16),
            pltpu.VMEM((ff, width), BF16),
            pltpu.VMEM((ff, tokens), BF16),
            pltpu.VMEM((tokens, width), BF16),
            pltpu.VMEM((tokens, 2 * ff), BF16),
            pltpu.VMEM((width, tokens), BF16),
            pltpu.VMEM((width, tokens), BF16),
            pltpu.VMEM((tokens, width), BF16),
            pltpu.VMEM((width, cols), BF16),
            pltpu.VMEM((ff, width), BF16),
            pltpu.SemaphoreType.DMA,
            pltpu.SemaphoreType.DMA,
        ],
        (order, order_g, flow, mid, gu, attended, gains, *w_a, *w_d),
        4 * tokens * width * (cols + ff),
        (width * cols + ff * width) * 4 + tokens * width * 16 + tokens * ff * 4,
    )


def attend_back_kernel(
    n_kv, low, bands, q_ref, do_ref, out_ref, lse_ref, row_ref, col_ref, cos_ref, sin_ref, *refs
):
    kv_refs = refs[:n_kv]
    dq_ref = refs[n_kv]
    dkv_refs = refs[n_kv + 1 : 2 * n_kv + 1]
    kv_s, kt_s, dqt_s, dkv_s, dlow_s, delta_s, sem = refs[2 * n_kv + 1 :]
    tokens, width = q_ref.shape
    total = kv_s.shape[0]
    load_bands(bands, kv_refs, kv_s, sem)
    head_of = lax.broadcasted_iota(jnp.int32, (16, width), 1) // HEAD_DIM
    picks = (head_of == lax.broadcasted_iota(jnp.int32, (16, width), 0)).astype(BF16)
    product = do_ref[...].astype(F32) * out_ref[...].astype(F32)
    upper = product.astype(BF16)
    lower = (product - upper.astype(F32)).astype(BF16)
    delta_s[...] = dot_nt(picks, upper) + dot_nt(picks, lower)
    dkv_s[...] = jnp.zeros_like(dkv_s)
    wait_whole(kv_s, sem)
    transpose_into(kt_s, kv_s, 0, width, total)
    first = bands[0] * tokens

    def q_step(q_index, carry):
        q_at = pl.multiple_of(q_index * Q_TILE, Q_TILE)
        q_rows = pl.ds(q_at, Q_TILE)
        dqt_s[...] = jnp.zeros_like(dqt_s)
        mark_row = row_ref[0:1, q_rows]

        def k_step(k_index, inner):
            k_at = pl.multiple_of(k_index * K_TILE, K_TILE)
            k_rows = pl.ds(k_at, K_TILE)
            bias = bias_tile(col_ref[k_rows, :], mark_row, k_at, first + q_at, K_TILE, Q_TILE)
            bias = jnp.concatenate([bias, bias], 1)
            for pair in range(HEADS // 2):
                lanes = slice(128 * pair, 128 * pair + 128)
                v_lanes = slice(width + 128 * pair, width + 128 * pair + 128)
                queries = head_pair(q_ref[q_rows, lanes])
                d_out = head_pair(do_ref[q_rows, lanes])
                lse = jnp.concatenate(
                    [lse_ref[2 * pair + side : 2 * pair + side + 1, q_rows] for side in (0, 1)], 1
                )
                delta = jnp.concatenate(
                    [delta_s[2 * pair + side : 2 * pair + side + 1, q_rows] for side in (0, 1)], 1
                )
                scores = dot_nt(kv_s[k_rows, lanes], queries) + bias
                probs = jnp.exp(scores - lse)
                d_probs = dot_nt(kv_s[k_rows, v_lanes], d_out)
                d_scores = (probs * (d_probs - delta)).astype(BF16)
                dkv_s[k_rows, v_lanes] += dot(probs.astype(BF16), d_out)
                dkv_s[k_rows, lanes] += dot(d_scores, queries)
                for side in (0, 1):
                    heads = slice(128 * pair + 64 * side, 128 * pair + 64 * side + 64)
                    part = slice(Q_TILE * side, Q_TILE * side + Q_TILE)
                    dqt_s[heads, :] += dot(kt_s[heads, k_rows], d_scores[:, part])
            return inner

        high = (first + q_at + Q_TILE - 1) // K_TILE + 1
        lax.fori_loop(low[q_index], high, k_step, 0)
        cosine, sine = cos_ref[q_rows, :], sin_ref[q_rows, :]
        for pair in range(HEADS // 2):
            lanes = slice(128 * pair, 128 * pair + 128)
            block = dqt_s[lanes, :].T * HEAD_DIM**-0.5
            dq_ref[q_rows, lanes] = (block * cosine - swap_halves(block) * sine).astype(BF16)
        return carry

    lax.fori_loop(0, tokens // Q_TILE, q_step, 0)
    for index, ref in enumerate(dkv_refs):
        at = pl.multiple_of(bands[index + 1] * tokens, tokens)
        dlow_s[index] = dkv_s[pl.ds(at, tokens), :].astype(BF16)
        pltpu.make_async_copy(dlow_s.at[index], ref, sem).start()
    wait_whole(dlow_s, sem)


def attend_back(low, bands, queries, d_out, out, lse, mark_row, mark_col, cosine, sine, kv_list, total):
    tokens, width = queries.shape
    n_kv = len(kv_list)
    return call(
        functools.partial(attend_back_kernel, n_kv),
        "attend_back",
        (
            jax.ShapeDtypeStruct((tokens, width), BF16),
            *([jax.ShapeDtypeStruct((tokens, 2 * width), BF16)] * n_kv),
        ),
        [SMEM, SMEM] + [VMEM] * 8 + [ANY] * n_kv,
        (VMEM, *([ANY] * n_kv)),
        [
            pltpu.VMEM((total, 2 * width), BF16),
            pltpu.VMEM((width, total), BF16),
            pltpu.VMEM((width, Q_TILE), F32),
            pltpu.VMEM((total, 2 * width), F32),
            pltpu.VMEM((n_kv, tokens, 2 * width), BF16),
            pltpu.VMEM((16, tokens), F32),
            pltpu.SemaphoreType.DMA,
        ],
        (low, bands, queries, d_out, out, lse, mark_row, mark_col, cosine, sine, *kv_list),
        20 * tokens * total * width,
        total * width * 8 + tokens * width * 8,
    )


def pre_back_kernel(
    n_w, n_g, n_kv, order, order_g, x_ref, dq_ref, cos_ref, sin_ref, gains_ref, dmid_ref, ggain_ref, *refs
):
    dkv_refs, w_refs = refs[:n_kv], refs[n_kv : n_kv + n_w]
    refs = refs[n_kv + n_w :]
    flow_ref, g_refs = refs[0], refs[1 : 1 + n_g]
    w_s, hidt_s, dqkv_s, g_s, sem = refs[1 + n_g :]
    tokens, width = x_ref.shape
    start_weights(order, w_refs, w_s, sem)
    gain = gains_ref[0:1, :]
    tile = row_tile(tokens)
    wait_whole(w_s, sem)
    ggain = jnp.zeros((1, width), F32)
    for start in range(0, tokens, tile):
        at = slice(start, start + tile)
        x = x_ref[at, :].astype(F32)
        factor = lax.rsqrt(jnp.mean(x * x, -1, keepdims=True) + EPS)
        normed = x * factor
        hidt_s[:, at] = (normed * gain).T.astype(BF16)
        cosine, sine = cos_ref[at, :], sin_ref[at, :]
        dqkv_s[at, :width] = dq_ref[at, :]
        for col in range(0, 2 * width, 128):
            block = dkv_refs[0][at, col : col + 128].astype(F32)
            for ref in dkv_refs[1:]:
                block = block + ref[at, col : col + 128].astype(F32)
            if col < width:
                block = block * cosine - swap_halves(block) * sine
            dqkv_s[at, width + col : width + col + 128] = block.astype(BF16)
        d_hid = dot_nt(dqkv_s[at, :], w_s[:, : 3 * width])
        ggain = ggain + jnp.sum(d_hid * normed, 0, keepdims=True)
        shaped = d_hid * gain
        flow_ref[at, :] = dmid_ref[at, :] + factor * (
            shaped - normed * jnp.mean(shaped * normed, -1, keepdims=True)
        )
    row = lax.broadcasted_iota(jnp.int32, (128, width), 0)
    both = jnp.where(row == 0, ggain, jnp.where(row == 1, ggain_ref[0:1, :], 0.0))
    g_s[:, 3 * width :] = both.T.astype(BF16)

    def columns(step, carry):
        col = pl.multiple_of(step * 256, 256)
        g_s[:, pl.ds(col, 256)] = dot(hidt_s[...], dqkv_s[:, pl.ds(col, 256)]).astype(BF16)
        return carry

    lax.fori_loop(0, 3 * width // 256, columns, 0)
    send_out(order_g, g_s, g_refs, sem)
    wait_whole(g_s, sem)


def pre_back(order, order_g, parts, x, dq, cosine, sine, gains, d_mid, ggain, dkv_list, weights):
    tokens, width = x.shape
    cols = weights[0].shape[1]
    n_g, per, pieces = parts
    return call(
        functools.partial(pre_back_kernel, len(weights), n_g, len(dkv_list)),
        "pre_back",
        (
            jax.ShapeDtypeStruct((tokens, width), F32),
            *([jax.ShapeDtypeStruct((per, width // pieces, cols), BF16)] * n_g),
        ),
        [SMEM, SMEM] + [VMEM] * (7 + len(dkv_list)) + [ANY] * len(weights),
        (VMEM, *([ANY] * n_g)),
        [
            pltpu.VMEM((width, cols), BF16),
            pltpu.VMEM((width, tokens), BF16),
            pltpu.VMEM((tokens, 3 * width), BF16),
            pltpu.VMEM((width, cols), BF16),
            pltpu.SemaphoreType.DMA,
        ],
        (order, order_g, x, dq, cosine, sine, gains, d_mid, ggain, *dkv_list, *weights),
        4 * tokens * width * 3 * width,
        width * cols * 4 + tokens * width * 20,
    )


class Layout:
    def __init__(self, n_rows, n_seq, width, ff):
        self.n_rows, self.n_seq = n_rows, n_seq
        self.paired = n_rows % 2 == 0 and n_seq % 2 == 0
        self.ringed = (
            n_rows % 4 == 0 and (width // n_rows) % 16 == 0 and (ff // n_rows) % 16 == 0
        )

    def device(self, row, seq):
        return row * self.n_seq + seq

    def pairs(self, move):
        return [
            (self.device(row, seq), self.device(*move(row, seq)))
            for row in range(self.n_rows)
            for seq in range(self.n_seq)
        ]

    def send(self, value, move):
        return lax.ppermute(value, BOTH, self.pairs(move))

    def to_core(self, value):
        return self.send(value, lambda row, seq: (row ^ 1, seq))

    def to_y(self, value):
        return self.send(value, lambda row, seq: (row ^ 2, seq))

    def to_z(self, value):
        return self.send(value, lambda row, seq: ((row + 4) % self.n_rows, seq))

    def to_x(self, value):
        return self.send(value, lambda row, seq: (row, (seq + 1) % self.n_seq))

    def regroup(self, row, seq):
        if not self.paired:
            return (row, seq)
        return (row - row % 2 + seq % 2, (row % 2) * (self.n_seq // 2) + seq // 2)

    def into_groups(self, value):
        return self.send(value, self.regroup) if self.paired else value

    def out_of_groups(self, value):
        if not self.paired:
            return value
        back = [(there, here) for here, there in self.pairs(self.regroup)]
        return lax.ppermute(value, BOTH, back)

    def band(self, row, seq):
        if not self.paired:
            return seq
        return (seq % (self.n_seq // 2)) * 2 + row % 2

    def groups(self):
        places = {}
        for row in range(self.n_rows):
            for seq in range(self.n_seq):
                there = self.regroup(row, seq)
                places.setdefault(row, {})[seq] = self.device(*there)
        return [[places[row][seq] for seq in range(self.n_seq)] for row in range(self.n_rows)]


def on_device(n_rows, n_seq, *args):
    inputs, seg_start, w_q, w_k, w_v, w_o, w_g, w_u, w_d, norm_attn, norm_mlp, cotangent = args
    _, tokens, width = inputs.shape
    ff = w_g.shape[2]
    total = tokens * n_seq
    lay = Layout(n_rows, n_seq, width, ff)
    row_at, seq_at = lax.axis_index("rows"), lax.axis_index("seq")

    def bundles(layer):
        gains = jnp.stack([norm_attn[layer], norm_mlp[layer]], 1)
        gains = jnp.pad(gains, ((0, 0), (0, 126)))
        return (
            jnp.concatenate([w_q[layer], w_k[layer], w_v[layer], gains], 1),
            jnp.concatenate([w_o[layer], w_g[layer], w_u[layer]], 1),
            w_d[layer],
        )

    def gather(shard):
        if not lay.ringed:
            return [lax.all_gather(shard, "rows", axis=0, tiled=True)]
        here = [shard]
        while len(here) < n_rows // 4:
            here.append(lay.to_z(here[-1]))
        here = here + [lay.to_y(chunk) for chunk in here]
        return here + [lay.to_core(chunk) for chunk in here]

    if lay.ringed:
        depth = n_rows // 4
        order, order_g = [], []
        for core in (0, 1):
            for side in (0, 2):
                for hop in range(depth):
                    order.append(((row_at - 4 * hop) % n_rows) ^ core ^ side)
                    order_g.append(((row_at + 4 * hop) % n_rows) ^ core ^ side)
        order, order_g = jnp.stack(order).astype(jnp.int32), jnp.stack(order_g).astype(jnp.int32)
        parts = (4, depth, n_rows)
    else:
        order = order_g = jnp.zeros((1,), jnp.int32)
        parts = (1, 1, 1)

    def scatter(stacks):
        if not lay.ringed:
            summed = lax.psum_scatter(stacks[0][0], "rows", scatter_dimension=0, tiled=True)
            return lax.psum(summed, "seq").astype(F32)
        far = (stacks[1].astype(F32) + lay.to_core(stacks[3]).astype(F32)).astype(BF16)
        far = lay.to_y(far).astype(F32)
        near = stacks[0].astype(F32) + lay.to_core(stacks[2]).astype(F32)
        both = near + far
        depth = both.shape[0]
        moving = both[depth - 1].astype(BF16)
        for hop in range(depth - 2, -1, -1):
            moving = (lay.to_z(moving).astype(F32) + both[hop]).astype(BF16)
        if n_seq != 2:
            return lax.psum(moving, "seq").astype(F32)
        return moving.astype(F32) + lay.to_x(moving).astype(F32)

    x_in = lay.into_groups(inputs[0])
    starts_mine = lay.into_groups(seg_start[0])
    d_top = lay.into_groups(cotangent[0])
    groups = lay.groups()
    half = n_seq // 2
    band = (seq_at % half) * 2 + row_at % 2 if lay.paired else seq_at
    two = lay.paired and n_seq == 2

    def exchange(value):
        if two:
            return [value, lay.to_core(value)]
        whole = lax.all_gather(value, BOTH, axis=0, axis_index_groups=groups)
        return [whole[index] for index in range(n_seq)]

    if two:
        bands = jnp.stack([band, band, 1 - band]).astype(jnp.int32)
    else:
        bands = jnp.concatenate([band[None], jnp.arange(n_seq)]).astype(jnp.int32)

    index = band * tokens + jnp.arange(tokens, dtype=jnp.int32)
    positions = jnp.where(starts_mine >= 0, index - starts_mine, 0)
    inverse = THETA ** (-jnp.arange(HEAD_DIM // 2, dtype=F32) * 2.0 / HEAD_DIM)
    angles = positions.astype(F32)[:, None] * inverse
    cosine = jnp.tile(jnp.cos(angles), (1, 4))
    sine = jnp.sin(angles)
    sine = jnp.concatenate([-sine, sine, -sine, sine], 1)
    marks = jnp.where(starts_mine >= 0, starts_mine, -1 - index)
    mark_row = jnp.broadcast_to(marks[None, :], (8, tokens))
    pieces = exchange(marks)
    if two:
        marks_all = jnp.where(
            band == 0, jnp.concatenate(pieces), jnp.concatenate([pieces[1], pieces[0]])
        )
    else:
        marks_all = jnp.concatenate(pieces)
    mark_col = jnp.broadcast_to(marks_all[:, None], (total, 128))
    reach = jnp.where(starts_mine >= 0, starts_mine, index)
    low = (jnp.min(reach.reshape(-1, Q_TILE), 1) // K_TILE).astype(jnp.int32)

    kept = []
    current = x_in
    for layer in range(LAYERS):
        qkv_shard, ogu_shard, down_shard = bundles(layer)
        w_qkv = gather(qkv_shard)
        w_ogu = gather(ogu_shard)
        w_down = gather(down_shard)
        queries, kv, gains = pre(order, current, cosine, sine, w_qkv)
        kv_list = exchange(kv)
        attended, lse = attend(low, bands, queries, mark_row, mark_col, kv_list, total)
        following, mid, gu = post(order, current, attended, gains, w_ogu, w_down)
        kept.append((current, queries, kv_list, attended, lse, mid, gu, gains, w_qkv, w_ogu, w_down))
        current = following
    output = lay.out_of_groups(current)

    grads = [None] * LAYERS
    flow = d_top
    for layer in reversed(range(LAYERS)):
        x, queries, kv_list, attended, lse, mid, gu, gains, w_qkv, w_ogu, w_down = kept[layer]
        n_g = parts[0]
        results = mlp_back(order, order_g, parts, flow, mid, gu, attended, gains, w_ogu, w_down)
        d_mid, d_att, ggain = results[:3]
        g_ogu = scatter(results[3 : 3 + n_g])
        g_down = scatter(results[3 + n_g : 3 + 2 * n_g])
        results = attend_back(
            low,
            bands,
            queries,
            d_att,
            attended,
            lse,
            mark_row,
            mark_col,
            cosine,
            sine,
            kv_list,
            total,
        )
        dq, dkv = results[0], results[1:]
        if two:
            dkv_list = [dkv[0], lay.to_core(dkv[1])]
        else:
            dkv_list = [
                lax.psum_scatter(
                    jnp.stack(dkv), BOTH, scatter_dimension=0, axis_index_groups=groups
                )
            ]
        results = pre_back(
            order, order_g, parts, x, dq, cosine, sine, gains, d_mid, ggain, dkv_list, w_qkv
        )
        flow = results[0]
        g_qkv = scatter(results[1:])
        grads[layer] = (g_qkv, g_ogu, g_down)
    grad_input = lay.out_of_groups(flow)

    def stack(which, first, size):
        return jnp.stack([grads[layer][which][:, first : first + size] for layer in range(LAYERS)])

    return (
        output[None],
        grad_input[None],
        stack(0, 0, width),
        stack(0, width, width),
        stack(0, 2 * width, width),
        stack(1, 0, width),
        stack(1, width, ff),
        stack(1, width + ff, ff),
        stack(2, 0, width),
        stack(0, 3 * width, 1)[..., 0],
        stack(0, 3 * width + 1, 1)[..., 0],
    )


def solution(mesh):
    rows3, rows2 = P("rows", "seq", None), P("rows", "seq")
    weight, vector = P(None, "rows", None), P(None, "rows")
    return jax.shard_map(
        functools.partial(on_device, mesh.shape["rows"], mesh.shape["seq"]),
        mesh=mesh,
        in_specs=(rows3, rows2, *([weight] * 7), vector, vector, rows3),
        out_specs=(rows3, rows3, *([weight] * 7), vector, vector),
        check_vma=False,
    )
```

```python
import functools

import jax
import jax.numpy as jnp
from jax import lax
from jax.experimental import pallas as pl
from jax.experimental.pallas import tpu as pltpu
from jax.sharding import PartitionSpec as P

HEADS = 12
HEAD_DIM = 64
LAYERS = 2
EPS = 1e-05
NEG_BIG = -1e30
THETA = 10000.0
F32 = jnp.float32
BF16 = jnp.bfloat16
BOTH = ("rows", "seq")
SMEM = pl.BlockSpec(memory_space=pltpu.SMEM)
VMEM = pl.BlockSpec(memory_space=pltpu.VMEM)
ANY = pl.BlockSpec(memory_space=pl.ANY)
VMEM_BYTES = 56 * 1024 * 1024
Q_TILE = 128
K_TILE = 256
FLOPS_PER_US = 1.1e9
IN_PARTS = (
    ([(1.0, "whole")], [(0.5, "whole"), (0.5, "half")], [(1.0, "half")]),
    ([(1.0, "half")], [(1.0, "whole")], [(1.0, "half")]),
)
OUT_PARTS = (
    ([(0.5, "whole"), (0.5, "half")], [(1.0, "offload")], [(1.0, "half")]),
    ([(1.0, "half")], [(1.0, "offload")], [(1.0, "half")]),
)


def dot(left, right):
    return jnp.dot(left, right, preferred_element_type=F32)


def dot_nt(left, right):
    return lax.dot_general(left, right, (((1,), (1,)), ((), ())), preferred_element_type=F32)


def swap_halves(block):
    lane = lax.broadcasted_iota(jnp.int32, block.shape, 1)
    return jnp.where(lane % 64 < 32, pltpu.roll(block, 96, 1), pltpu.roll(block, 32, 1))


def place(table, index, rows, cols, whole):
    at = pl.ds(pl.multiple_of(table[0, index] * rows, 16), rows)
    if cols == whole.shape[1]:
        return whole.at[at, :]
    return whole.at[at, pl.ds(pl.multiple_of(table[1, index] * 128, 128), cols)]


def start_weights(table, refs, held, sem):
    index = 0
    for ref in refs:
        for part in range(ref.shape[0]):
            target = place(table, index, ref.shape[1], ref.shape[2], held)
            pltpu.make_async_copy(ref.at[part], target, sem).start()
            index += 1


def wait_whole(held, sem):
    pltpu.make_async_copy(held, held, sem).wait()


def send_out(table, whole, refs, sem):
    index = 0
    for ref in refs:
        for part in range(ref.shape[0]):
            source = place(table, index, ref.shape[1], ref.shape[2], whole)
            pltpu.make_async_copy(source, ref.at[part], sem).start()
            index += 1


def call(kernel, name, out_shape, in_specs, out_specs, scratch, args, micros, ride=(), before=()):
    n_in, n_out, n_ride = len(in_specs), len(out_specs), len(ride)
    n_more = n_ride + len(before)

    def wrapped(*refs):
        outs_at = n_in + n_more
        kernel(*refs[:n_in], *refs[outs_at : outs_at + n_out], *refs[outs_at + n_out + n_ride :])

    results = pl.pallas_call(
        wrapped,
        name=name,
        out_shape=(*out_shape, *(jax.ShapeDtypeStruct(a.shape, a.dtype) for a in ride)),
        in_specs=[*in_specs, *([ANY] * n_more)],
        out_specs=(*out_specs, *([ANY] * n_ride)),
        scratch_shapes=scratch,
        input_output_aliases={n_in + i: n_out + i for i in range(n_ride)},
        compiler_params=pltpu.CompilerParams(vmem_limit_bytes=VMEM_BYTES),
        cost_estimate=pl.CostEstimate(
            flops=int(micros * FLOPS_PER_US), bytes_accessed=0, transcendentals=0
        ),
    )(*args, *ride, *before)
    return results[:n_out], list(results[n_out:])


def qkv_cols(width):
    return 3 * width + 256


def row_tile(tokens):
    return min(256, tokens)


def pre_kernel(n_w, order, x_ref, cos_ref, sin_ref, *refs):
    w_refs = refs[:n_w]
    q_ref, kv_ref, gains_ref, w_s, hid_s, sem = refs[n_w:]
    tokens, width = x_ref.shape
    start_weights(order, w_refs, w_s, sem)
    wait_whole(w_s, sem)
    gains_ref[...] = w_s[:, 3 * width : 3 * width + 128].astype(F32).T[:8]
    gain = gains_ref[0:1, :]
    tile = row_tile(tokens)

    def body(step, carry):
        at = pl.ds(pl.multiple_of(step * tile, tile), tile)
        x = x_ref[at, :].astype(F32)
        factor = lax.rsqrt(jnp.mean(x * x, -1, keepdims=True) + EPS)
        hidden = (x * factor * gain).astype(BF16)
        cosine, sine = cos_ref[at, :], sin_ref[at, :]
        for col in range(0, 3 * width, 256):
            part = dot(hidden, w_s[:, col : col + 256])
            if col < 2 * width:
                halves = []
                for lane in (0, 128):
                    block = part[:, lane : lane + 128]
                    halves.append(block * cosine + swap_halves(block) * sine)
                part = jnp.concatenate(halves, 1)
            if col < width:
                q_ref[at, col : col + 256] = (part * HEAD_DIM**-0.5).astype(BF16)
            else:
                kv_ref[at, col - width : col - width + 256] = part.astype(BF16)
        return carry

    lax.fori_loop(0, tokens // tile, body, 0)


def pre(order, x, cosine, sine, weights, ride=(), before=()):
    tokens, width = x.shape
    cols = qkv_cols(width)
    return call(
        functools.partial(pre_kernel, len(weights)),
        "pre",
        (
            jax.ShapeDtypeStruct((tokens, width), BF16),
            jax.ShapeDtypeStruct((tokens, 2 * width), BF16),
            jax.ShapeDtypeStruct((8, width), F32),
        ),
        [SMEM, VMEM, VMEM, VMEM] + [ANY] * len(weights),
        (VMEM, VMEM, VMEM),
        [
            pltpu.VMEM((width, cols), BF16),
            pltpu.VMEM((tokens, width), BF16),
            pltpu.SemaphoreType.DMA,
        ],
        (order, x, cosine, sine, *weights),
        7,
        ride,
        before,
    )


def gate_kernel(done_ref):
    done_ref[...] = jnp.zeros_like(done_ref)


def gate(before, ride):
    return call(
        gate_kernel, "gate", (jax.ShapeDtypeStruct((8, 128), F32),), [], (VMEM,), [], (), 0, ride, before
    )[1]


def load_bands(bands, kv_refs, kv_s, sem):
    tokens = kv_refs[0].shape[0]
    for index, ref in enumerate(kv_refs):
        at = pl.multiple_of(bands[index + 1] * tokens, tokens)
        pltpu.make_async_copy(ref, kv_s.at[pl.ds(at, tokens), :], sem).start()


def bias_tile(mark_col, mark_row, k_at, q_at, k_tile, q_tile):
    key = k_at + lax.broadcasted_iota(jnp.int32, (k_tile, q_tile), 0)
    query = q_at + lax.broadcasted_iota(jnp.int32, (k_tile, q_tile), 1)
    return jnp.where((mark_col == mark_row) & (key <= query), 0.0, NEG_BIG)


def head_pair(block):
    lane = lax.broadcasted_iota(jnp.int32, block.shape, 1)
    zero = jnp.zeros_like(block)
    return jnp.concatenate(
        [jnp.where(lane < 64, block, zero), jnp.where(lane >= 64, block, zero)], 0
    )


def transpose_into(dest, source, first, columns, rows):
    for col in range(0, columns, 128):
        for row in range(0, rows, 128):
            block = source[row : row + 128, first + col : first + col + 128]
            dest[col : col + 128, row : row + 128] = block.astype(F32).T.astype(BF16)


def attend_kernel(n_kv, low, bands, q_ref, row_ref, col_ref, *refs):
    kv_refs = refs[:n_kv]
    out_ref, lse_ref, kv_s, vt_s, acc_s, max_s, sum_s, sem = refs[n_kv:]
    tokens, width = q_ref.shape
    total = kv_s.shape[0]
    load_bands(bands, kv_refs, kv_s, sem)
    wait_whole(kv_s, sem)
    transpose_into(vt_s, kv_s, width, width, total)
    first = bands[0] * tokens
    lse_ref[...] = jnp.zeros_like(lse_ref)

    def q_step(q_index, carry):
        q_at = pl.multiple_of(q_index * Q_TILE, Q_TILE)
        max_s[...] = jnp.full_like(max_s, NEG_BIG)
        sum_s[...] = jnp.zeros_like(sum_s)
        acc_s[...] = jnp.zeros_like(acc_s)
        mark_row = row_ref[0:1, pl.ds(q_at, Q_TILE)]

        def k_step(k_index, inner):
            k_at = pl.multiple_of(k_index * K_TILE, K_TILE)
            bias = bias_tile(
                col_ref[pl.ds(k_at, K_TILE), :], mark_row, k_at, first + q_at, K_TILE, Q_TILE
            )
            bias = jnp.concatenate([bias, bias], 1)
            for pair in range(HEADS // 2):
                lanes = slice(128 * pair, 128 * pair + 128)
                queries = head_pair(q_ref[pl.ds(q_at, Q_TILE), lanes])
                scores = dot_nt(kv_s[pl.ds(k_at, K_TILE), lanes], queries) + bias
                before = max_s[pair : pair + 1, :]
                highest = jnp.maximum(before, jnp.max(scores, 0, keepdims=True))
                shrink = jnp.exp(before - highest)
                expd = jnp.exp(scores - highest)
                max_s[pair : pair + 1, :] = highest
                sum_s[pair : pair + 1, :] = sum_s[pair : pair + 1, :] * shrink + jnp.sum(
                    expd, 0, keepdims=True
                )
                low_p = expd.astype(BF16)
                for side in (0, 1):
                    heads = slice(128 * pair + 64 * side, 128 * pair + 64 * side + 64)
                    part = slice(Q_TILE * side, Q_TILE * side + Q_TILE)
                    mixed = dot(vt_s[heads, pl.ds(k_at, K_TILE)], low_p[:, part])
                    acc_s[heads, :] = acc_s[heads, :] * shrink[:, part] + mixed
            return inner

        high = (first + q_at + Q_TILE - 1) // K_TILE + 1
        lax.fori_loop(low[q_index], high, k_step, 0)
        for pair in range(HEADS // 2):
            lanes = slice(128 * pair, 128 * pair + 128)
            scale = 1.0 / sum_s[pair : pair + 1, :]
            lse = max_s[pair : pair + 1, :] + jnp.log(sum_s[pair : pair + 1, :])
            both = []
            for side in (0, 1):
                heads = slice(128 * pair + 64 * side, 128 * pair + 64 * side + 64)
                part = slice(Q_TILE * side, Q_TILE * side + Q_TILE)
                both.append(acc_s[heads, :] * scale[:, part])
                row = 2 * pair + side
                lse_ref[row : row + 1, pl.ds(q_at, Q_TILE)] = lse[:, part]
            out_ref[pl.ds(q_at, Q_TILE), lanes] = jnp.concatenate(both, 0).T.astype(BF16)
        return carry

    lax.fori_loop(0, tokens // Q_TILE, q_step, 0)


def attend(low, bands, queries, mark_row, mark_col, kv_list, total, ride=(), before=()):
    tokens, width = queries.shape
    return call(
        functools.partial(attend_kernel, len(kv_list)),
        "attend",
        (
            jax.ShapeDtypeStruct((tokens, width), BF16),
            jax.ShapeDtypeStruct((16, tokens), F32),
        ),
        [SMEM, SMEM, VMEM, VMEM, VMEM] + [ANY] * len(kv_list),
        (VMEM, VMEM),
        [
            pltpu.VMEM((total, 2 * width), BF16),
            pltpu.VMEM((width, total), BF16),
            pltpu.VMEM((width, Q_TILE), F32),
            pltpu.VMEM((8, 2 * Q_TILE), F32),
            pltpu.VMEM((8, 2 * Q_TILE), F32),
            pltpu.SemaphoreType.DMA,
        ],
        (low, bands, queries, mark_row, mark_col, *kv_list),
        15,
        ride,
        before,
    )


def post_kernel(n_a, n_d, order_a, order_d, x_ref, att_ref, gains_ref, *refs):
    a_refs, d_refs = refs[:n_a], refs[n_a : n_a + n_d]
    out_ref, mid_ref, gu_ref, a_s, d_s, act_s, sem_a, sem_d = refs[n_a + n_d :]
    tokens, width = x_ref.shape
    ff = d_s.shape[0]
    start_weights(order_a, a_refs, a_s, sem_a)
    start_weights(order_d, d_refs, d_s, sem_d)
    wait_whole(a_s, sem_a)
    wait_whole(d_s, sem_d)
    gain = gains_ref[1:2, :]
    tile = row_tile(tokens)

    def body(step, carry):
        at = pl.ds(pl.multiple_of(step * tile, tile), tile)
        mid = x_ref[at, :].astype(F32) + dot(att_ref[at, :], a_s[:, :width])
        mid_ref[at, :] = mid
        factor = lax.rsqrt(jnp.mean(mid * mid, -1, keepdims=True) + EPS)
        hidden = (mid * factor * gain).astype(BF16)
        for col in range(0, ff, 256):
            gate = dot(hidden, a_s[:, width + col : width + col + 256])
            up = dot(hidden, a_s[:, width + ff + col : width + ff + col + 256])
            gu_ref[at, col : col + 256] = gate.astype(BF16)
            gu_ref[at, ff + col : ff + col + 256] = up.astype(BF16)
            act_s[:, col : col + 256] = (gate * jax.nn.sigmoid(gate) * up).astype(BF16)
        out_ref[at, :] = mid + dot(act_s[...], d_s[...])
        return carry

    lax.fori_loop(0, tokens // tile, body, 0)


def post(order_a, order_d, ff, x, attended, gains, w_a, w_d, ride=(), before=()):
    tokens, width = x.shape
    cols = width + 2 * ff
    return call(
        functools.partial(post_kernel, len(w_a), len(w_d)),
        "post",
        (
            jax.ShapeDtypeStruct((tokens, width), F32),
            jax.ShapeDtypeStruct((tokens, width), F32),
            jax.ShapeDtypeStruct((tokens, 2 * ff), BF16),
        ),
        [SMEM, SMEM, VMEM, VMEM, VMEM] + [ANY] * (len(w_a) + len(w_d)),
        (VMEM, VMEM, VMEM),
        [
            pltpu.VMEM((width, cols), BF16),
            pltpu.VMEM((ff, width), BF16),
            pltpu.VMEM((row_tile(tokens), ff), BF16),
            pltpu.SemaphoreType.DMA,
            pltpu.SemaphoreType.DMA,
        ],
        (order_a, order_d, x, attended, gains, *w_a, *w_d),
        14,
        ride,
        before,
    )


def mlp_back_kernel(
    counts, order_d, table_a, table_d, flow_ref, mid_ref, gu_ref, gains_ref, *refs
):
    n_d, n_ga, n_gd = counts
    d_refs, refs = refs[:n_d], refs[n_d:]
    dgu_ref, ga_refs, gd_refs = refs[0], refs[1 : 1 + n_ga], refs[1 + n_ga : 1 + n_ga + n_gd]
    d_s, actt_s, db_s, hidt_s, ga_s, gd_s, sem_a, sem_d = refs[1 + n_ga + n_gd :]
    tokens, width = mid_ref.shape
    ff = d_s.shape[0]
    start_weights(order_d, d_refs, d_s, sem_d)
    gain = gains_ref[1:2, :]
    tile = row_tile(tokens)
    for start in range(0, tokens, tile):
        at = slice(start, start + tile)
        db_s[at, :] = flow_ref[at, :].astype(BF16)
        mid = mid_ref[at, :]
        factor = lax.rsqrt(jnp.mean(mid * mid, -1, keepdims=True) + EPS)
        hidt_s[:, at] = (mid * factor * gain).T.astype(BF16)
    wait_whole(d_s, sem_d)

    def columns(step, carry):
        col = pl.multiple_of(step * 256, 256)
        for start in range(0, tokens, tile):
            at = slice(start, start + tile)
            d_act = dot_nt(db_s[at, :], d_s[pl.ds(col, 256), :])
            gate = gu_ref[at, pl.ds(col, 256)].astype(F32)
            up = gu_ref[at, pl.ds(ff + col, 256)].astype(F32)
            sigma = jax.nn.sigmoid(gate)
            silu = gate * sigma
            actt_s[pl.ds(col, 256), at] = (silu * up).T.astype(BF16)
            dgu_ref[at, pl.ds(col, 256)] = (
                d_act * up * (sigma * (1.0 + gate * (1.0 - sigma)))
            ).astype(BF16)
            dgu_ref[at, pl.ds(ff + col, 256)] = (d_act * silu).astype(BF16)
        for first in (0, ff):
            ga_s[:, pl.ds(first + col, 256)] = dot(
                hidt_s[...], dgu_ref[:, pl.ds(first + col, 256)]
            ).astype(BF16)
        rows = pl.ds(col, 256)
        gd_s[rows, :] = dot(actt_s[rows, :], db_s[...]).astype(BF16)
        return carry

    lax.fori_loop(0, ff // 256, columns, 0)
    send_out(table_a, ga_s, ga_refs, sem_a)
    send_out(table_d, gd_s, gd_refs, sem_d)
    wait_whole(ga_s, sem_a)
    wait_whole(gd_s, sem_d)


def mlp_back(order_d, tables, shapes, flow, mid, gu, gains, w_d, ride=(), before=()):
    tokens, width = mid.shape
    ff = gu.shape[1] // 2
    ga, gd = shapes
    return call(
        functools.partial(mlp_back_kernel, (len(w_d), len(ga), len(gd))),
        "mlp_back",
        (jax.ShapeDtypeStruct((tokens, 2 * ff), BF16), *ga, *gd),
        [SMEM] * 3 + [VMEM] * 4 + [ANY] * len(w_d),
        (VMEM, *([ANY] * (len(ga) + len(gd)))),
        [
            pltpu.VMEM((ff, width), BF16),
            pltpu.VMEM((ff, tokens), BF16),
            pltpu.VMEM((tokens, width), BF16),
            pltpu.VMEM((width, tokens), BF16),
            pltpu.VMEM((width, 2 * ff), BF16),
            pltpu.VMEM((ff, width), BF16),
            pltpu.SemaphoreType.DMA,
            pltpu.SemaphoreType.DMA,
        ],
        (order_d, *tables, flow, mid, gu, gains, *w_d),
        20,
        ride,
        before,
    )


def mid_back_kernel(n_a, order_a, flow_ref, mid_ref, dgu_ref, gains_ref, *refs):
    a_refs = refs[:n_a]
    dmid_ref, dattn_ref, datt_ref, ggain_ref, a_s, sem = refs[n_a:]
    tokens, width = mid_ref.shape
    start_weights(order_a, a_refs, a_s, sem)
    gain = gains_ref[1:2, :]
    tile = row_tile(tokens)
    wait_whole(a_s, sem)
    ggain = jnp.zeros((1, width), F32)
    for start in range(0, tokens, tile):
        at = slice(start, start + tile)
        mid = mid_ref[at, :]
        factor = lax.rsqrt(jnp.mean(mid * mid, -1, keepdims=True) + EPS)
        normed = mid * factor
        d_hid = dot_nt(dgu_ref[at, :], a_s[:, width:])
        ggain = ggain + jnp.sum(d_hid * normed, 0, keepdims=True)
        shaped = d_hid * gain
        d_mid = flow_ref[at, :].astype(F32) + factor * (
            shaped - normed * jnp.mean(shaped * normed, -1, keepdims=True)
        )
        dmid_ref[at, :] = d_mid
        d_attn = d_mid.astype(BF16)
        dattn_ref[at, :] = d_attn
        datt_ref[at, :] = dot_nt(d_attn, a_s[:, :width]).astype(BF16)
    ggain_ref[...] = jnp.broadcast_to(ggain, ggain_ref.shape)


def mid_back(order_a, flow, mid, dgu, gains, w_a, ride=(), before=()):
    tokens, width = mid.shape
    return call(
        functools.partial(mid_back_kernel, len(w_a)),
        "mid_back",
        (
            jax.ShapeDtypeStruct((tokens, width), F32),
            jax.ShapeDtypeStruct((tokens, width), BF16),
            jax.ShapeDtypeStruct((tokens, width), BF16),
            jax.ShapeDtypeStruct((8, width), F32),
        ),
        [SMEM] + [VMEM] * 4 + [ANY] * len(w_a),
        (VMEM, VMEM, VMEM, VMEM),
        [
            pltpu.VMEM((width, width + dgu.shape[1]), BF16),
            pltpu.SemaphoreType.DMA,
        ],
        (order_a, flow, mid, dgu, gains, *w_a),
        13,
        ride,
        before,
    )


def attend_back_kernel(
    n_kv, low, bands, q_ref, do_ref, out_ref, lse_ref, row_ref, col_ref, cos_ref, sin_ref, *refs
):
    kv_refs = refs[:n_kv]
    dq_ref = refs[n_kv]
    dkv_refs = refs[n_kv + 1 : 2 * n_kv + 1]
    kv_s, kt_s, dqt_s, dkv_s, dlow_s, delta_s, sem = refs[2 * n_kv + 1 :]
    tokens, width = q_ref.shape
    total = kv_s.shape[0]
    load_bands(bands, kv_refs, kv_s, sem)
    head_of = lax.broadcasted_iota(jnp.int32, (16, width), 1) // HEAD_DIM
    picks = (head_of == lax.broadcasted_iota(jnp.int32, (16, width), 0)).astype(BF16)
    product = do_ref[...].astype(F32) * out_ref[...].astype(F32)
    upper = product.astype(BF16)
    lower = (product - upper.astype(F32)).astype(BF16)
    delta_s[...] = dot_nt(picks, upper) + dot_nt(picks, lower)
    dkv_s[...] = jnp.zeros_like(dkv_s)
    wait_whole(kv_s, sem)
    transpose_into(kt_s, kv_s, 0, width, total)
    first = bands[0] * tokens

    def q_step(q_index, carry):
        q_at = pl.multiple_of(q_index * Q_TILE, Q_TILE)
        q_rows = pl.ds(q_at, Q_TILE)
        dqt_s[...] = jnp.zeros_like(dqt_s)
        mark_row = row_ref[0:1, q_rows]

        def k_step(k_index, inner):
            k_at = pl.multiple_of(k_index * K_TILE, K_TILE)
            k_rows = pl.ds(k_at, K_TILE)
            bias = bias_tile(col_ref[k_rows, :], mark_row, k_at, first + q_at, K_TILE, Q_TILE)
            bias = jnp.concatenate([bias, bias], 1)
            for pair in range(HEADS // 2):
                lanes = slice(128 * pair, 128 * pair + 128)
                v_lanes = slice(width + 128 * pair, width + 128 * pair + 128)
                queries = head_pair(q_ref[q_rows, lanes])
                d_out = head_pair(do_ref[q_rows, lanes])
                lse = jnp.concatenate(
                    [lse_ref[2 * pair + side : 2 * pair + side + 1, q_rows] for side in (0, 1)], 1
                )
                delta = jnp.concatenate(
                    [delta_s[2 * pair + side : 2 * pair + side + 1, q_rows] for side in (0, 1)], 1
                )
                scores = dot_nt(kv_s[k_rows, lanes], queries) + bias
                probs = jnp.exp(scores - lse)
                d_probs = dot_nt(kv_s[k_rows, v_lanes], d_out)
                d_scores = (probs * (d_probs - delta)).astype(BF16)
                dkv_s[k_rows, v_lanes] += dot(probs.astype(BF16), d_out)
                dkv_s[k_rows, lanes] += dot(d_scores, queries)
                for side in (0, 1):
                    heads = slice(128 * pair + 64 * side, 128 * pair + 64 * side + 64)
                    part = slice(Q_TILE * side, Q_TILE * side + Q_TILE)
                    dqt_s[heads, :] += dot(kt_s[heads, k_rows], d_scores[:, part])
            return inner

        high = (first + q_at + Q_TILE - 1) // K_TILE + 1
        lax.fori_loop(low[q_index], high, k_step, 0)
        cosine, sine = cos_ref[q_rows, :], sin_ref[q_rows, :]
        for pair in range(HEADS // 2):
            lanes = slice(128 * pair, 128 * pair + 128)
            block = dqt_s[lanes, :].T * HEAD_DIM**-0.5
            dq_ref[q_rows, lanes] = (block * cosine - swap_halves(block) * sine).astype(BF16)
        return carry

    lax.fori_loop(0, tokens // Q_TILE, q_step, 0)
    for index, ref in enumerate(dkv_refs):
        at = pl.multiple_of(bands[index + 1] * tokens, tokens)
        dlow_s[index] = dkv_s[pl.ds(at, tokens), :].astype(BF16)
        pltpu.make_async_copy(dlow_s.at[index], ref, sem).start()
    wait_whole(dlow_s, sem)


def attend_back(low, bands, queries, d_out, out, lse, mark_row, mark_col, cosine, sine, kv_list, total, ride=(), before=()):
    tokens, width = queries.shape
    n_kv = len(kv_list)
    return call(
        functools.partial(attend_back_kernel, n_kv),
        "attend_back",
        (
            jax.ShapeDtypeStruct((tokens, width), BF16),
            *([jax.ShapeDtypeStruct((tokens, 2 * width), BF16)] * n_kv),
        ),
        [SMEM, SMEM] + [VMEM] * 8 + [ANY] * n_kv,
        (VMEM, *([ANY] * n_kv)),
        [
            pltpu.VMEM((total, 2 * width), BF16),
            pltpu.VMEM((width, total), BF16),
            pltpu.VMEM((width, Q_TILE), F32),
            pltpu.VMEM((total, 2 * width), F32),
            pltpu.VMEM((n_kv, tokens, 2 * width), BF16),
            pltpu.VMEM((16, tokens), F32),
            pltpu.SemaphoreType.DMA,
        ],
        (low, bands, queries, d_out, out, lse, mark_row, mark_col, cosine, sine, *kv_list),
        20,
        ride,
        before,
    )


def pre_back_kernel(
    n_w,
    n_g,
    n_kv,
    order,
    table,
    x_ref,
    dq_ref,
    cos_ref,
    sin_ref,
    gains_ref,
    dmid_ref,
    ggain_ref,
    att_ref,
    dattn_ref,
    *refs,
):
    dkv_refs, w_refs = refs[:n_kv], refs[n_kv : n_kv + n_w]
    refs = refs[n_kv + n_w :]
    flow_ref, g_refs = refs[0], refs[1 : 1 + n_g]
    w_s, hidt_s, dqkv_s, attt_s, g_s, sem = refs[1 + n_g :]
    tokens, width = x_ref.shape
    start_weights(order, w_refs, w_s, sem)
    gain = gains_ref[0:1, :]
    tile = row_tile(tokens)
    wait_whole(w_s, sem)
    ggain = jnp.zeros((1, width), F32)
    for start in range(0, tokens, tile):
        at = slice(start, start + tile)
        x = x_ref[at, :].astype(F32)
        factor = lax.rsqrt(jnp.mean(x * x, -1, keepdims=True) + EPS)
        normed = x * factor
        hidt_s[:, at] = (normed * gain).T.astype(BF16)
        attt_s[:, at] = att_ref[at, :].astype(F32).T.astype(BF16)
        cosine, sine = cos_ref[at, :], sin_ref[at, :]
        dqkv_s[at, :width] = dq_ref[at, :]
        for col in range(0, 2 * width, 128):
            block = dkv_refs[0][at, col : col + 128].astype(F32)
            for ref in dkv_refs[1:]:
                block = block + ref[at, col : col + 128].astype(F32)
            if col < width:
                block = block * cosine - swap_halves(block) * sine
            dqkv_s[at, width + col : width + col + 128] = block.astype(BF16)
        d_hid = dot_nt(dqkv_s[at, :], w_s[:, : 3 * width])
        ggain = ggain + jnp.sum(d_hid * normed, 0, keepdims=True)
        shaped = d_hid * gain
        flow_ref[at, :] = dmid_ref[at, :] + factor * (
            shaped - normed * jnp.mean(shaped * normed, -1, keepdims=True)
        )
    row = lax.broadcasted_iota(jnp.int32, (128, width), 0)
    both = jnp.where(row == 0, ggain, jnp.where(row == 1, ggain_ref[0:1, :], 0.0))
    g_s[:, 4 * width : 4 * width + 128] = both.T.astype(BF16)
    g_s[:, 4 * width + 128 :] = jnp.zeros((width, 128), BF16)
    g_s[:, 3 * width : 4 * width] = dot(attt_s[...], dattn_ref[...]).astype(BF16)

    def columns(step, carry):
        col = pl.multiple_of(step * 256, 256)
        g_s[:, pl.ds(col, 256)] = dot(hidt_s[...], dqkv_s[:, pl.ds(col, 256)]).astype(BF16)
        return carry

    lax.fori_loop(0, 3 * width // 256, columns, 0)
    send_out(table, g_s, g_refs, sem)
    wait_whole(g_s, sem)


def pre_back(
    order,
    table,
    shapes,
    x,
    dq,
    cosine,
    sine,
    gains,
    d_mid,
    ggain,
    attended,
    d_attn,
    dkv_list,
    weights,
    ride=(),
    before=(),
):
    tokens, width = x.shape
    return call(
        functools.partial(pre_back_kernel, len(weights), len(shapes), len(dkv_list)),
        "pre_back",
        (jax.ShapeDtypeStruct((tokens, width), F32), *shapes),
        [SMEM, SMEM] + [VMEM] * (9 + len(dkv_list)) + [ANY] * len(weights),
        (VMEM, *([ANY] * len(shapes))),
        [
            pltpu.VMEM((width, qkv_cols(width)), BF16),
            pltpu.VMEM((width, tokens), BF16),
            pltpu.VMEM((tokens, 3 * width), BF16),
            pltpu.VMEM((width, tokens), BF16),
            pltpu.VMEM((width, width + qkv_cols(width)), BF16),
            pltpu.SemaphoreType.DMA,
        ],
        (
            order,
            table,
            x,
            dq,
            cosine,
            sine,
            gains,
            d_mid,
            ggain,
            attended,
            d_attn,
            *dkv_list,
            *weights,
        ),
        15,
        ride,
        before,
    )


class Layout:
    def __init__(self, n_rows, n_seq, width, ff):
        self.n_rows, self.n_seq = n_rows, n_seq
        self.paired = n_rows % 2 == 0 and n_seq % 2 == 0
        self.ringed = (
            n_rows % 4 == 0 and (width // n_rows) % 16 == 0 and (ff // n_rows) % 16 == 0
        )

    def device(self, row, seq):
        return row * self.n_seq + seq

    def pairs(self, move):
        return [
            (self.device(row, seq), self.device(*move(row, seq)))
            for row in range(self.n_rows)
            for seq in range(self.n_seq)
        ]

    def send(self, value, move):
        return lax.ppermute(value, BOTH, self.pairs(move))

    def to_core(self, value):
        return self.send(value, lambda row, seq: (row ^ 1, seq))

    def to_y(self, value):
        return self.send(value, lambda row, seq: (row ^ 2, seq))

    def to_z(self, value, hops):
        return self.send(value, lambda row, seq: ((row + 4 * hops) % self.n_rows, seq))

    def to_x(self, value):
        return self.send(value, lambda row, seq: (row, (seq + 1) % self.n_seq))

    def regroup(self, row, seq):
        if not self.paired:
            return (row, seq)
        return (row - row % 2 + seq % 2, (row % 2) * (self.n_seq // 2) + seq // 2)

    def into_groups(self, value):
        return self.send(value, self.regroup) if self.paired else value

    def out_of_groups(self, value):
        if not self.paired:
            return value
        back = [(there, here) for here, there in self.pairs(self.regroup)]
        return lax.ppermute(value, BOTH, back)

    def band(self, row, seq):
        if not self.paired:
            return seq
        return (seq % (self.n_seq // 2)) * 2 + row % 2

    def groups(self):
        places = {}
        for row in range(self.n_rows):
            for seq in range(self.n_seq):
                there = self.regroup(row, seq)
                places.setdefault(row, {})[seq] = self.device(*there)
        return [[places[row][seq] for seq in range(self.n_seq)] for row in range(self.n_rows)]


def on_device(n_rows, n_seq, *args):
    inputs, seg_start, w_q, w_k, w_v, w_o, w_g, w_u, w_d, norm_attn, norm_mlp, cotangent = args
    _, tokens, width = inputs.shape
    ff = w_g.shape[2]
    total = tokens * n_seq
    lay = Layout(n_rows, n_seq, width, ff)
    row_at, seq_at = lax.axis_index("rows"), lax.axis_index("seq")
    ringed = lay.ringed and n_seq == 2
    depth = n_rows // 4

    def bundles(layer):
        gains = jnp.stack([norm_attn[layer], norm_mlp[layer]], 1)
        gains = jnp.pad(gains, ((0, 0), (0, 254)))
        return [
            jnp.concatenate([w_q[layer], w_k[layer], w_v[layer], gains], 1),
            jnp.concatenate([w_o[layer], w_g[layer], w_u[layer]], 1),
            w_d[layer],
        ]

    def split(cols, parts):
        if not ringed:
            return [(0, cols, "offload")]
        found, first = [], 0
        for count, (share, mode) in enumerate(parts, 1):
            size = cols - first if count == len(parts) else round(cols * share / 256) * 256
            found.append((first, size, mode))
            first += size
        return found

    def table(sign, pieces):
        numbers, columns = [], []
        for first, size, mode in pieces:
            if mode == "offload":
                numbers.append(jnp.int32(0))
                columns.append(jnp.int32(first // 128))
                continue
            for core in (0, 1):
                for half in (0, 1) if mode == "half" else (0,):
                    for side in (0, 2):
                        for hop in range(depth):
                            numbers.append(((row_at + sign * 4 * hop) % n_rows) ^ core ^ side)
                            columns.append(
                                first // 128 + (seq_at ^ half) * (size // 256)
                                if mode == "half"
                                else jnp.int32(first // 128)
                            )
        return jnp.stack([jnp.stack(numbers), jnp.stack(columns)]).astype(jnp.int32)

    def shapes(rows, pieces):
        found = []
        for _, size, mode in pieces:
            if mode == "offload":
                found.append(jax.ShapeDtypeStruct((1, rows, size), BF16))
            elif mode == "half":
                found += [jax.ShapeDtypeStruct((2 * depth, rows // n_rows, size // 2), BF16)] * 4
            else:
                found += [jax.ShapeDtypeStruct((depth, rows // n_rows, size), BF16)] * 4
        return found

    def up(value):
        return value.astype(F32)

    class Gather:
        def __init__(self, shard, mode):
            self.mode, self.stacks, self.level = mode, None, 0
            if mode == "offload":
                self.stacks = [lax.all_gather(shard, "rows", axis=0, tiled=True)[None]]
                return
            if mode == "half":
                columns = shard.shape[1] // 2
                shard = lax.dynamic_slice_in_dim(shard, seq_at * columns, columns, 1)
            self.stay, self.flying = [shard], []
            while len(self.flying) + 1 < depth:
                self.flying.append(lay.to_z((self.stay + self.flying)[-1], 1))

        def step(self):
            self.level += 1
            if self.stacks is not None:
                return
            if self.level == 1:
                near = jnp.stack(self.stay + self.flying)
                self.stay, self.flying = [near], [lay.to_y(near)]
            elif self.level == 2 and self.mode == "whole":
                near, far = self.stay[0], self.flying[0]
                self.stacks = [near, far, lay.to_core(near), lay.to_core(far)]
            elif self.level == 2:
                both = jnp.concatenate([self.stay[0], self.flying[0]])
                self.stay, self.flying = [both], [lay.to_x(both)]
            else:
                both, other = self.stay[0], self.flying[0]
                self.stacks = [both, other, lay.to_core(both), lay.to_core(other)]

        def finish(self):
            while self.stacks is None:
                self.step()
            return self.stacks

    class Scatter:
        def __init__(self, stack, mode):
            self.mode, self.sum, self.level, self.old = mode, None, 0, False
            if mode == "offload":
                summed = lax.psum_scatter(stack[0][0], "rows", scatter_dimension=0, tiled=True)
                if n_seq == 2:
                    self.stay, self.flying, self.level = [summed], [lay.to_x(summed)], 9
                else:
                    self.sum = up(lax.psum(summed, "seq"))
                return
            self.flying = [lay.to_core(stack[3]), lay.to_core(stack[2])]
            self.stay = [stack[1], stack[0]]

        def along_z(self, both):
            sent = [both[hop].astype(BF16) for hop in range(1, depth)]
            self.flying = [lay.to_z(value, hop) for hop, value in enumerate(sent, 1)]
            self.stay = [both[0]]
            return sent

        def step(self):
            if self.sum is not None:
                return []
            self.level += 1
            half = self.mode == "half"
            stay, flying = self.stay, self.flying
            if self.level == 1:
                first = (up(stay[0]) + up(flying[0])).astype(BF16)
                self.stay = [stay[1]]
                self.flying = [lay.to_x(first) if half else lay.to_y(first), flying[1]]
                return [first]
            if self.level == 2:
                both = up(stay[0]) + up(flying[1]) + up(flying[0])
                if not half:
                    return self.along_z(both)
                far = both[depth:].astype(BF16)
                self.stay, self.flying = [both[:depth]], [lay.to_y(far)]
                return [far]
            if self.level == 3 and half:
                return self.along_z(stay[0] + up(flying[0]))
            if self.level == (4 if half else 3):
                total = up(stay[0])
                for value in flying:
                    total = total + up(value)
                total = total.astype(BF16)
                self.stay, self.flying = [total], [lay.to_x(total)]
                return [total]
            mine, other = stay[0], flying[0]
            if not half:
                self.sum = up(mine) + up(other)
                return []
            self.sum = up(
                jnp.where(
                    seq_at == 0,
                    jnp.concatenate([mine, other], 1),
                    jnp.concatenate([other, mine], 1),
                )
            )
            return []

        def finish(self):
            while self.sum is None:
                self.step()
            return self.sum

    def scatters(arrays, pieces):
        found, at = [], 0
        for _, _, mode in pieces:
            size = 1 if mode == "offload" else 4
            found.append(Scatter(arrays[at : at + size], mode))
            at += size
        return found

    def joined(chains):
        sums = [chain.finish() for chain in chains]
        return sums[0] if len(sums) == 1 else jnp.concatenate(sums, 1)

    x_in = lay.into_groups(inputs[0])
    starts_mine = lay.into_groups(seg_start[0])
    d_top = lay.into_groups(cotangent[0])
    groups = lay.groups()
    half_seq = n_seq // 2
    band = (seq_at % half_seq) * 2 + row_at % 2 if lay.paired else seq_at
    two = lay.paired and n_seq == 2

    def exchange(value):
        if two:
            return [value, lay.to_core(value)]
        whole = lax.all_gather(value, BOTH, axis=0, axis_index_groups=groups)
        return [whole[index] for index in range(n_seq)]

    if two:
        bands = jnp.stack([band, band, 1 - band]).astype(jnp.int32)
    else:
        bands = jnp.concatenate([band[None], jnp.arange(n_seq)]).astype(jnp.int32)

    index = band * tokens + jnp.arange(tokens, dtype=jnp.int32)
    positions = jnp.where(starts_mine >= 0, index - starts_mine, 0)
    inverse = THETA ** (-jnp.arange(HEAD_DIM // 2, dtype=F32) * 2.0 / HEAD_DIM)
    angles = positions.astype(F32)[:, None] * inverse
    cosine = jnp.tile(jnp.cos(angles), (1, 4))
    sine = jnp.sin(angles)
    sine = jnp.concatenate([-sine, sine, -sine, sine], 1)
    marks = jnp.where(starts_mine >= 0, starts_mine, -1 - index)
    mark_row = jnp.broadcast_to(marks[None, :], (8, tokens))
    pieces = exchange(marks)
    if two:
        marks_all = jnp.where(
            band == 0, jnp.concatenate(pieces), jnp.concatenate([pieces[1], pieces[0]])
        )
    else:
        marks_all = jnp.concatenate(pieces)
    mark_col = jnp.broadcast_to(marks_all[:, None], (total, 128))
    reach = jnp.where(starts_mine >= 0, starts_mine, index)
    low = (jnp.min(reach.reshape(-1, Q_TILE), 1) // K_TILE).astype(jnp.int32)

    in_widths = (qkv_cols(width), width + 2 * ff, width)
    out_widths = (width + qkv_cols(width), 2 * ff, width)
    in_pieces = [[split(c, p) for c, p in zip(in_widths, parts)] for parts in IN_PARTS]
    out_pieces = [[split(c, p) for c, p in zip(out_widths, parts)] for parts in OUT_PARTS]
    known = {}

    def table_of(sign, pieces):
        key = (sign, *pieces)
        if key not in known:
            known[key] = table(sign, pieces)
        return known[key]

    orders = [[table_of(-1, pieces) for pieces in in_pieces[layer]] for layer in range(LAYERS)]
    tables = [[table_of(1, pieces) for pieces in out_pieces[layer]] for layer in range(LAYERS)]

    def gathers(shard, pieces):
        return [Gather(shard[:, first : first + size], mode) for first, size, mode in pieces]

    def arrived(chains):
        return [stack for chain in chains for stack in chain.finish()]

    kept = []
    current = x_in
    weights = []

    def near_of(bundles_of_chains):
        found = []
        for chains_here in bundles_of_chains:
            for chain in chains_here:
                if chain.stacks is None:
                    chain.step()
                    found += chain.stay
        return found

    shards = bundles(0)
    moving = [[gathers(shards[0], in_pieces[0][0])], None]
    if ringed:
        _ = ([value for chain in moving[0][0] for value in chain.flying], shards[1:])
    moving[0] += [gathers(s, p) for s, p in zip(shards[1:], in_pieces[0][1:])]
    for layer in range(LAYERS):
        last = layer + 1 == LAYERS
        o_qkv, o_ogu, o_down = orders[layer]
        w_qkv = arrived(moving[layer][0])
        (queries, kv, gains), ridden = pre(
            o_qkv,
            current,
            cosine,
            sine,
            w_qkv,
            ride=[] if last else bundles(layer + 1),
        )
        kv_list = exchange(kv)
        (attended, lse), _ = attend(
            low,
            bands,
            queries,
            mark_row,
            mark_col,
            kv_list,
            total,
        )
        before = []
        if not last:
            moving[layer + 1] = [gathers(s, p) for s, p in zip(ridden, in_pieces[layer + 1])]
        w_ogu, w_down = arrived(moving[layer][1]), arrived(moving[layer][2])
        (result, mid, gu), _ = post(
            o_ogu, o_down, ff, current, attended, gains, w_ogu, w_down, before=before
        )
        kept.append((current, queries, kv_list, attended, lse, mid, gu, gains))
        weights.append((w_qkv, w_ogu, w_down))
        current = result
    output = lay.out_of_groups(current.astype(BF16)).astype(F32)

    flow = d_top
    chains = [None] * LAYERS
    live = []

    def through(kernel, *args, **more):
        if not ringed:
            return kernel(*args, **more)[0]
        sent = more.pop("before", [])
        for chain in live:
            if chain.level < 9:
                sent = sent + (chain.step() if chain.old else [])
            chain.old = True
        holders = [chain for chain in live if chain.sum is None and chain.level < 9]
        ride = [value for chain in holders for value in chain.stay]
        results, ridden = kernel(*args, ride=ride, before=sent, **more)
        for chain in holders:
            chain.stay, ridden = ridden[: len(chain.stay)], ridden[len(chain.stay) :]
        return results

    for layer in reversed(range(LAYERS)):
        x, queries, kv_list, attended, lse, mid, gu, gains = kept[layer]
        o_qkv, o_ogu, o_down = orders[layer]
        w_qkv, w_ogu, w_down = weights[layer]
        t_qkv, t_gu, t_down = tables[layer]
        p_qkv, p_gu, p_down = out_pieces[layer]
        s_gu, s_down = shapes(width, p_gu), shapes(ff, p_down)
        results = through(
            mlp_back, o_down, (t_gu, t_down), (s_gu, s_down), flow, mid, gu, gains, w_down
        )
        dgu = results[0]
        c_gu = scatters(results[1 : 1 + len(s_gu)], p_gu)
        c_down = scatters(results[1 + len(s_gu) :], p_down)
        live += c_gu + c_down
        d_mid, d_attn, d_att, ggain = through(mid_back, o_ogu, flow, mid, dgu, gains, w_ogu)
        results = through(
            attend_back,
            low,
            bands,
            queries,
            d_att,
            attended,
            lse,
            mark_row,
            mark_col,
            cosine,
            sine,
            kv_list,
            total,
        )
        dq, dkv = results[0], results[1:]
        if two:
            dkv_list = [dkv[0], lay.to_core(dkv[1])]
        else:
            dkv_list = [
                lax.psum_scatter(
                    jnp.stack(dkv), BOTH, scatter_dimension=0, axis_index_groups=groups
                )
            ]
        s_qkv = shapes(width, p_qkv)
        results = through(
            pre_back,
            o_qkv,
            t_qkv,
            s_qkv,
            x,
            dq,
            cosine,
            sine,
            gains,
            d_mid,
            ggain,
            attended,
            d_attn,
            dkv_list,
            w_qkv,
            before=[output] if layer == 0 else [],
        )
        flow = results[0]
        c_qkv = scatters(results[1:], p_qkv)
        live += c_qkv
        chains[layer] = (c_qkv, c_gu, c_down)
    while ringed and any(chain.sum is None and chain.level < 9 for chain in live):
        through(lambda ride, before: ([], gate(before, ride)))
    grads = [[joined(part) for part in chains[layer]] for layer in range(LAYERS)]
    grad_input = lay.out_of_groups(flow.astype(BF16)).astype(F32)

    def stack(which, first, size):
        return jnp.stack([grads[layer][which][:, first : first + size] for layer in range(LAYERS)])

    return (
        output[None],
        grad_input[None],
        stack(0, 0, width),
        stack(0, width, width),
        stack(0, 2 * width, width),
        stack(0, 3 * width, width),
        stack(1, 0, ff),
        stack(1, ff, ff),
        stack(2, 0, width),
        stack(0, 4 * width, 1)[..., 0],
        stack(0, 4 * width + 1, 1)[..., 0],
    )


def solution(mesh):
    rows3, rows2 = P("rows", "seq", None), P("rows", "seq")
    weight, vector = P(None, "rows", None), P(None, "rows")
    return jax.shard_map(
        functools.partial(on_device, mesh.shape["rows"], mesh.shape["seq"]),
        mesh=mesh,
        in_specs=(rows3, rows2, *([weight] * 7), vector, vector, rows3),
        out_specs=(rows3, rows3, *([weight] * 7), vector, vector),
        check_vma=False,
    )
```

```python
import functools

import jax
import jax.numpy as jnp
from jax import lax
from jax.experimental import pallas as pl
from jax.experimental.pallas import tpu as pltpu
from jax.sharding import PartitionSpec as P

HEADS = 12
HEAD_DIM = 64
LAYERS = 2
EPS = 1e-05
NEG_BIG = -1e30
THETA = 10000.0
F32 = jnp.float32
BF16 = jnp.bfloat16
BOTH = ("rows", "seq")
SMEM = pl.BlockSpec(memory_space=pltpu.SMEM)
VMEM = pl.BlockSpec(memory_space=pltpu.VMEM)
ANY = pl.BlockSpec(memory_space=pl.ANY)
VMEM_MIB = dict(
    gate=2, pre=18, attend=14, post=32, mlp_back=38, mid_back=28, attend_back=28, pre_back=34
)
Q_TILE, K_TILE = 128, 128
Q_BACK, K_BACK = 256, 256
FLOPS_PER_US = 1.1e9
IN_PARTS = (
    ([(1.0, "whole")], [(0.5, "whole"), (0.5, "half")], [(1.0, "half")]),
    ([(1.0, "half")], [(1.0, "whole")], [(1.0, "half")]),
)
OUT_PARTS = (
    ([(0.5, "whole"), (0.5, "half")], [(1.0, "offload")], [(1.0, "half")]),
    ([(1.0, "half")], [(1.0, "offload")], [(1.0, "half")]),
)


def dot(left, right):
    return jnp.dot(left, right, preferred_element_type=F32)


def dot_nt(left, right):
    return lax.dot_general(left, right, (((1,), (1,)), ((), ())), preferred_element_type=F32)


def swap_halves(block):
    lane = lax.broadcasted_iota(jnp.int32, block.shape, 1)
    return jnp.where(lane % 64 < 32, pltpu.roll(block, 96, 1), pltpu.roll(block, 32, 1))


def place(table, index, rows, cols, whole):
    at = pl.ds(pl.multiple_of(table[0, index] * rows, 16), rows)
    if cols == whole.shape[1]:
        return whole.at[at, :]
    return whole.at[at, pl.ds(pl.multiple_of(table[1, index] * 128, 128), cols)]


def start_weights(table, refs, held, sem):
    index = 0
    for ref in refs:
        for part in range(ref.shape[0]):
            target = place(table, index, ref.shape[1], ref.shape[2], held)
            pltpu.make_async_copy(ref.at[part], target, sem).start()
            index += 1


def wait_whole(held, sem):
    pltpu.make_async_copy(held, held, sem).wait()


def send_out(table, whole, refs, sem):
    index = 0
    for ref in refs:
        for part in range(ref.shape[0]):
            source = place(table, index, ref.shape[1], ref.shape[2], whole)
            pltpu.make_async_copy(source, ref.at[part], sem).start()
            index += 1


def call(kernel, name, out_shape, in_specs, out_specs, scratch, args, micros, ride=(), before=()):
    n_in, n_out, n_ride = len(in_specs), len(out_specs), len(ride)
    n_more = n_ride + len(before)

    def wrapped(*refs):
        outs_at = n_in + n_more
        kernel(*refs[:n_in], *refs[outs_at : outs_at + n_out], *refs[outs_at + n_out + n_ride :])

    results = pl.pallas_call(
        wrapped,
        name=name,
        out_shape=(*out_shape, *(jax.ShapeDtypeStruct(a.shape, a.dtype) for a in ride)),
        in_specs=[*in_specs, *([ANY] * n_more)],
        out_specs=(*out_specs, *([ANY] * n_ride)),
        scratch_shapes=scratch,
        input_output_aliases={n_in + i: n_out + i for i in range(n_ride)},
        compiler_params=pltpu.CompilerParams(vmem_limit_bytes=VMEM_MIB[name] * 1024 * 1024),
        cost_estimate=pl.CostEstimate(
            flops=int(micros * FLOPS_PER_US), bytes_accessed=0, transcendentals=0
        ),
    )(*args, *ride, *before)
    return results[:n_out], list(results[n_out:])


def qkv_cols(width):
    return 3 * width + 256


def row_tile(tokens):
    return min(256, tokens)


def pre_kernel(n_w, order, x_ref, cos_ref, sin_ref, *refs):
    w_refs = refs[:n_w]
    q_ref, kv_ref, gains_ref, w_s, hid_s, sem = refs[n_w:]
    tokens, width = x_ref.shape
    start_weights(order, w_refs, w_s, sem)
    wait_whole(w_s, sem)
    gains_ref[...] = w_s[:, 3 * width : 3 * width + 128].astype(F32).T[:8]
    gain = gains_ref[0:1, :]
    tile = row_tile(tokens)

    def body(step, carry):
        at = pl.ds(pl.multiple_of(step * tile, tile), tile)
        x = x_ref[at, :].astype(F32)
        factor = lax.rsqrt(jnp.mean(x * x, -1, keepdims=True) + EPS)
        hidden = (x * factor * gain).astype(BF16)
        cosine, sine = cos_ref[at, :], sin_ref[at, :]
        for col in range(0, 3 * width, 256):
            part = dot(hidden, w_s[:, col : col + 256])
            if col < 2 * width:
                halves = []
                for lane in (0, 128):
                    block = part[:, lane : lane + 128]
                    halves.append(block * cosine + swap_halves(block) * sine)
                part = jnp.concatenate(halves, 1)
            if col < width:
                q_ref[at, col : col + 256] = (part * HEAD_DIM**-0.5).astype(BF16)
            else:
                kv_ref[at, col - width : col - width + 256] = part.astype(BF16)
        return carry

    lax.fori_loop(0, tokens // tile, body, 0)


def pre(order, x, cosine, sine, weights, ride=(), before=()):
    tokens, width = x.shape
    cols = qkv_cols(width)
    return call(
        functools.partial(pre_kernel, len(weights)),
        "pre",
        (
            jax.ShapeDtypeStruct((tokens, width), BF16),
            jax.ShapeDtypeStruct((tokens, 2 * width), BF16),
            jax.ShapeDtypeStruct((8, width), F32),
        ),
        [SMEM, VMEM, VMEM, VMEM] + [ANY] * len(weights),
        (VMEM, VMEM, VMEM),
        [
            pltpu.VMEM((width, cols), BF16),
            pltpu.VMEM((tokens, width), BF16),
            pltpu.SemaphoreType.DMA,
        ],
        (order, x, cosine, sine, *weights),
        7,
        ride,
        before,
    )


def gate_kernel(done_ref):
    done_ref[...] = jnp.zeros_like(done_ref)


def gate(before, ride):
    return call(
        gate_kernel, "gate", (jax.ShapeDtypeStruct((8, 128), F32),), [], (VMEM,), [], (), 0, ride, before
    )[1]


def load_bands(bands, kv_refs, kv_s, sem):
    tokens = kv_refs[0].shape[0]
    for index, ref in enumerate(kv_refs):
        at = pl.multiple_of(bands[index + 1] * tokens, tokens)
        pltpu.make_async_copy(ref, kv_s.at[pl.ds(at, tokens), :], sem).start()


def bias_tile(mark_col, mark_row, k_at, q_at, k_tile, q_tile):
    key = k_at + lax.broadcasted_iota(jnp.int32, (k_tile, q_tile), 0)
    query = q_at + lax.broadcasted_iota(jnp.int32, (k_tile, q_tile), 1)
    return jnp.where((mark_col == mark_row) & (key <= query), 0.0, NEG_BIG)


def head_pair(block):
    lane = lax.broadcasted_iota(jnp.int32, block.shape, 1)
    zero = jnp.zeros_like(block)
    return jnp.concatenate(
        [jnp.where(lane < 64, block, zero), jnp.where(lane >= 64, block, zero)], 0
    )


def transpose_tiles(dest, source, first, columns, low, high, k_tile):
    def body(tile, carry):
        at = pl.ds(pl.multiple_of(tile * k_tile, k_tile), k_tile)
        for col in range(0, columns, 128):
            block = source[at, first + col : first + col + 128]
            dest[col : col + 128, at] = block.astype(F32).T.astype(BF16)
        return carry

    lax.fori_loop(low, high, body, 0)


def attend_kernel(n_kv, low, bands, q_ref, row_ref, col_ref, *refs):
    kv_refs = refs[:n_kv]
    out_ref, lse_ref, kv_s, vt_s, acc_s, max_s, sum_s, sem = refs[n_kv:]
    tokens, width = q_ref.shape
    total = kv_s.shape[0]
    load_bands(bands, kv_refs, kv_s, sem)
    wait_whole(kv_s, sem)
    first = bands[0] * tokens
    transpose_tiles(vt_s, kv_s, width, width, low[0] // K_TILE, (first + tokens - 1) // K_TILE + 1, K_TILE)
    lse_ref[...] = jnp.zeros_like(lse_ref)

    def q_step(q_index, carry):
        q_at = pl.multiple_of(q_index * Q_TILE, Q_TILE)
        max_s[...] = jnp.full_like(max_s, NEG_BIG)
        sum_s[...] = jnp.zeros_like(sum_s)
        acc_s[...] = jnp.zeros_like(acc_s)
        mark_row = row_ref[0:1, pl.ds(q_at, Q_TILE)]

        def k_step(k_index, inner):
            k_at = pl.multiple_of(k_index * K_TILE, K_TILE)
            bias = bias_tile(
                col_ref[pl.ds(k_at, K_TILE), :], mark_row, k_at, first + q_at, K_TILE, Q_TILE
            )
            bias = jnp.concatenate([bias, bias], 1)
            for pair in range(HEADS // 2):
                lanes = slice(128 * pair, 128 * pair + 128)
                queries = head_pair(q_ref[pl.ds(q_at, Q_TILE), lanes])
                scores = dot_nt(kv_s[pl.ds(k_at, K_TILE), lanes], queries) + bias
                before = max_s[pair : pair + 1, :]
                highest = jnp.maximum(before, jnp.max(scores, 0, keepdims=True))
                shrink = jnp.exp(before - highest)
                expd = jnp.exp(scores - highest)
                max_s[pair : pair + 1, :] = highest
                sum_s[pair : pair + 1, :] = sum_s[pair : pair + 1, :] * shrink + jnp.sum(
                    expd, 0, keepdims=True
                )
                low_p = expd.astype(BF16)
                for side in (0, 1):
                    heads = slice(128 * pair + 64 * side, 128 * pair + 64 * side + 64)
                    part = slice(Q_TILE * side, Q_TILE * side + Q_TILE)
                    mixed = dot(vt_s[heads, pl.ds(k_at, K_TILE)], low_p[:, part])
                    acc_s[heads, :] = acc_s[heads, :] * shrink[:, part] + mixed
            return inner

        high = (first + q_at + Q_TILE - 1) // K_TILE + 1
        lax.fori_loop(low[q_index] // K_TILE, high, k_step, 0)
        for pair in range(HEADS // 2):
            lanes = slice(128 * pair, 128 * pair + 128)
            scale = 1.0 / sum_s[pair : pair + 1, :]
            lse = max_s[pair : pair + 1, :] + jnp.log(sum_s[pair : pair + 1, :])
            both = []
            for side in (0, 1):
                heads = slice(128 * pair + 64 * side, 128 * pair + 64 * side + 64)
                part = slice(Q_TILE * side, Q_TILE * side + Q_TILE)
                both.append(acc_s[heads, :] * scale[:, part])
                row = 2 * pair + side
                lse_ref[row : row + 1, pl.ds(q_at, Q_TILE)] = lse[:, part]
            out_ref[pl.ds(q_at, Q_TILE), lanes] = jnp.concatenate(both, 0).T.astype(BF16)
        return carry

    lax.fori_loop(0, tokens // Q_TILE, q_step, 0)


def attend(low, bands, queries, mark_row, mark_col, kv_list, total, ride=(), before=()):
    tokens, width = queries.shape
    return call(
        functools.partial(attend_kernel, len(kv_list)),
        "attend",
        (
            jax.ShapeDtypeStruct((tokens, width), BF16),
            jax.ShapeDtypeStruct((16, tokens), F32),
        ),
        [SMEM, SMEM, VMEM, VMEM, VMEM] + [ANY] * len(kv_list),
        (VMEM, VMEM),
        [
            pltpu.VMEM((total, 2 * width), BF16),
            pltpu.VMEM((width, total), BF16),
            pltpu.VMEM((width, Q_TILE), F32),
            pltpu.VMEM((8, 2 * Q_TILE), F32),
            pltpu.VMEM((8, 2 * Q_TILE), F32),
            pltpu.SemaphoreType.DMA,
        ],
        (low, bands, queries, mark_row, mark_col, *kv_list),
        15,
        ride,
        before,
    )


def post_kernel(n_a, n_d, order_a, order_d, x_ref, att_ref, gains_ref, *refs):
    a_refs, d_refs = refs[:n_a], refs[n_a : n_a + n_d]
    out_ref, mid_ref, gu_ref, a_s, d_s, act_s, sem_a, sem_d = refs[n_a + n_d :]
    tokens, width = x_ref.shape
    ff = d_s.shape[0]
    start_weights(order_a, a_refs, a_s, sem_a)
    start_weights(order_d, d_refs, d_s, sem_d)
    wait_whole(a_s, sem_a)
    wait_whole(d_s, sem_d)
    gain = gains_ref[1:2, :]
    tile = row_tile(tokens)

    def body(step, carry):
        at = pl.ds(pl.multiple_of(step * tile, tile), tile)
        mid = x_ref[at, :].astype(F32) + dot(att_ref[at, :], a_s[:, :width])
        mid_ref[at, :] = mid
        factor = lax.rsqrt(jnp.mean(mid * mid, -1, keepdims=True) + EPS)
        hidden = (mid * factor * gain).astype(BF16)
        for col in range(0, ff, 256):
            gate = dot(hidden, a_s[:, width + col : width + col + 256])
            up = dot(hidden, a_s[:, width + ff + col : width + ff + col + 256])
            gu_ref[at, col : col + 256] = gate.astype(BF16)
            gu_ref[at, ff + col : ff + col + 256] = up.astype(BF16)
            act_s[:, col : col + 256] = (gate * jax.nn.sigmoid(gate) * up).astype(BF16)
        out_ref[at, :] = mid + dot(act_s[...], d_s[...])
        return carry

    lax.fori_loop(0, tokens // tile, body, 0)


def post(order_a, order_d, ff, x, attended, gains, w_a, w_d, ride=(), before=()):
    tokens, width = x.shape
    cols = width + 2 * ff
    return call(
        functools.partial(post_kernel, len(w_a), len(w_d)),
        "post",
        (
            jax.ShapeDtypeStruct((tokens, width), F32),
            jax.ShapeDtypeStruct((tokens, width), F32),
            jax.ShapeDtypeStruct((tokens, 2 * ff), BF16),
        ),
        [SMEM, SMEM, VMEM, VMEM, VMEM] + [ANY] * (len(w_a) + len(w_d)),
        (VMEM, VMEM, VMEM),
        [
            pltpu.VMEM((width, cols), BF16),
            pltpu.VMEM((ff, width), BF16),
            pltpu.VMEM((row_tile(tokens), ff), BF16),
            pltpu.SemaphoreType.DMA,
            pltpu.SemaphoreType.DMA,
        ],
        (order_a, order_d, x, attended, gains, *w_a, *w_d),
        14,
        ride,
        before,
    )


def mlp_back_kernel(
    counts, order_d, table_a, table_d, flow_ref, mid_ref, gu_ref, gains_ref, *refs
):
    n_d, n_ga, n_gd = counts
    d_refs, refs = refs[:n_d], refs[n_d:]
    dgu_ref, ga_refs, gd_refs = refs[0], refs[1 : 1 + n_ga], refs[1 + n_ga : 1 + n_ga + n_gd]
    d_s, actt_s, db_s, hidt_s, ga_s, gd_s, sem_a, sem_d = refs[1 + n_ga + n_gd :]
    tokens, width = mid_ref.shape
    ff = d_s.shape[0]
    start_weights(order_d, d_refs, d_s, sem_d)
    gain = gains_ref[1:2, :]
    tile = row_tile(tokens)
    for start in range(0, tokens, tile):
        at = slice(start, start + tile)
        db_s[at, :] = flow_ref[at, :].astype(BF16)
        mid = mid_ref[at, :]
        factor = lax.rsqrt(jnp.mean(mid * mid, -1, keepdims=True) + EPS)
        hidt_s[:, at] = (mid * factor * gain).T.astype(BF16)
    wait_whole(d_s, sem_d)

    def columns(step, carry):
        col = pl.multiple_of(step * 256, 256)
        for start in range(0, tokens, tile):
            at = slice(start, start + tile)
            d_act = dot_nt(db_s[at, :], d_s[pl.ds(col, 256), :])
            gate = gu_ref[at, pl.ds(col, 256)].astype(F32)
            up = gu_ref[at, pl.ds(ff + col, 256)].astype(F32)
            sigma = jax.nn.sigmoid(gate)
            silu = gate * sigma
            actt_s[pl.ds(col, 256), at] = (silu * up).T.astype(BF16)
            dgu_ref[at, pl.ds(col, 256)] = (
                d_act * up * (sigma * (1.0 + gate * (1.0 - sigma)))
            ).astype(BF16)
            dgu_ref[at, pl.ds(ff + col, 256)] = (d_act * silu).astype(BF16)
        for first in (0, ff):
            ga_s[:, pl.ds(first + col, 256)] = dot(
                hidt_s[...], dgu_ref[:, pl.ds(first + col, 256)]
            ).astype(BF16)
        rows = pl.ds(col, 256)
        gd_s[rows, :] = dot(actt_s[rows, :], db_s[...]).astype(BF16)
        return carry

    lax.fori_loop(0, ff // 256, columns, 0)
    send_out(table_a, ga_s, ga_refs, sem_a)
    send_out(table_d, gd_s, gd_refs, sem_d)
    wait_whole(ga_s, sem_a)
    wait_whole(gd_s, sem_d)


def mlp_back(order_d, tables, shapes, flow, mid, gu, gains, w_d, ride=(), before=()):
    tokens, width = mid.shape
    ff = gu.shape[1] // 2
    ga, gd = shapes
    return call(
        functools.partial(mlp_back_kernel, (len(w_d), len(ga), len(gd))),
        "mlp_back",
        (jax.ShapeDtypeStruct((tokens, 2 * ff), BF16), *ga, *gd),
        [SMEM] * 3 + [VMEM] * 4 + [ANY] * len(w_d),
        (VMEM, *([ANY] * (len(ga) + len(gd)))),
        [
            pltpu.VMEM((ff, width), BF16),
            pltpu.VMEM((ff, tokens), BF16),
            pltpu.VMEM((tokens, width), BF16),
            pltpu.VMEM((width, tokens), BF16),
            pltpu.VMEM((width, 2 * ff), BF16),
            pltpu.VMEM((ff, width), BF16),
            pltpu.SemaphoreType.DMA,
            pltpu.SemaphoreType.DMA,
        ],
        (order_d, *tables, flow, mid, gu, gains, *w_d),
        20,
        ride,
        before,
    )


def mid_back_kernel(n_a, order_a, flow_ref, mid_ref, dgu_ref, gains_ref, *refs):
    a_refs = refs[:n_a]
    dmid_ref, dattn_ref, datt_ref, ggain_ref, a_s, sem = refs[n_a:]
    tokens, width = mid_ref.shape
    start_weights(order_a, a_refs, a_s, sem)
    gain = gains_ref[1:2, :]
    tile = row_tile(tokens)
    wait_whole(a_s, sem)
    ggain = jnp.zeros((1, width), F32)
    for start in range(0, tokens, tile):
        at = slice(start, start + tile)
        mid = mid_ref[at, :]
        factor = lax.rsqrt(jnp.mean(mid * mid, -1, keepdims=True) + EPS)
        normed = mid * factor
        d_hid = dot_nt(dgu_ref[at, :], a_s[:, width:])
        ggain = ggain + jnp.sum(d_hid * normed, 0, keepdims=True)
        shaped = d_hid * gain
        d_mid = flow_ref[at, :].astype(F32) + factor * (
            shaped - normed * jnp.mean(shaped * normed, -1, keepdims=True)
        )
        dmid_ref[at, :] = d_mid
        d_attn = d_mid.astype(BF16)
        dattn_ref[at, :] = d_attn
        datt_ref[at, :] = dot_nt(d_attn, a_s[:, :width]).astype(BF16)
    ggain_ref[...] = jnp.broadcast_to(ggain, ggain_ref.shape)


def mid_back(order_a, flow, mid, dgu, gains, w_a, ride=(), before=()):
    tokens, width = mid.shape
    return call(
        functools.partial(mid_back_kernel, len(w_a)),
        "mid_back",
        (
            jax.ShapeDtypeStruct((tokens, width), F32),
            jax.ShapeDtypeStruct((tokens, width), BF16),
            jax.ShapeDtypeStruct((tokens, width), BF16),
            jax.ShapeDtypeStruct((8, width), F32),
        ),
        [SMEM] + [VMEM] * 4 + [ANY] * len(w_a),
        (VMEM, VMEM, VMEM, VMEM),
        [
            pltpu.VMEM((width, width + dgu.shape[1]), BF16),
            pltpu.SemaphoreType.DMA,
        ],
        (order_a, flow, mid, dgu, gains, *w_a),
        13,
        ride,
        before,
    )


def attend_back_kernel(
    n_kv, low, bands, q_ref, do_ref, out_ref, lse_ref, row_ref, col_ref, cos_ref, sin_ref, *refs
):
    kv_refs = refs[:n_kv]
    dq_ref = refs[n_kv]
    dkv_refs = refs[n_kv + 1 : 2 * n_kv + 1]
    kv_s, kt_s, dqt_s, dkv_s, dlow_s, delta_s, sem = refs[2 * n_kv + 1 :]
    tokens, width = q_ref.shape
    q_tile = min(Q_BACK, tokens)
    total = kv_s.shape[0]
    load_bands(bands, kv_refs, kv_s, sem)
    head_of = lax.broadcasted_iota(jnp.int32, (16, width), 1) // HEAD_DIM
    picks = (head_of == lax.broadcasted_iota(jnp.int32, (16, width), 0)).astype(BF16)
    product = do_ref[...].astype(F32) * out_ref[...].astype(F32)
    upper = product.astype(BF16)
    lower = (product - upper.astype(F32)).astype(BF16)
    delta_s[...] = dot_nt(picks, upper) + dot_nt(picks, lower)
    dkv_s[...] = jnp.zeros_like(dkv_s)
    wait_whole(kv_s, sem)
    first = bands[0] * tokens
    transpose_tiles(kt_s, kv_s, 0, width, low[0] // K_BACK, (first + tokens - 1) // K_BACK + 1, K_BACK)

    def q_step(q_index, carry):
        q_at = pl.multiple_of(q_index * q_tile, q_tile)
        q_rows = pl.ds(q_at, q_tile)
        dqt_s[...] = jnp.zeros_like(dqt_s)
        mark_row = row_ref[0:1, q_rows]

        def k_step(k_index, inner):
            k_at = pl.multiple_of(k_index * K_BACK, K_BACK)
            k_rows = pl.ds(k_at, K_BACK)
            bias = bias_tile(col_ref[k_rows, 0:1], mark_row, k_at, first + q_at, K_BACK, q_tile)
            bias = jnp.concatenate([bias, bias], 1)
            for pair in range(HEADS // 2):
                lanes = slice(128 * pair, 128 * pair + 128)
                v_lanes = slice(width + 128 * pair, width + 128 * pair + 128)
                queries = head_pair(q_ref[q_rows, lanes])
                d_out = head_pair(do_ref[q_rows, lanes])
                lse = jnp.concatenate(
                    [lse_ref[2 * pair + side : 2 * pair + side + 1, q_rows] for side in (0, 1)], 1
                )
                delta = jnp.concatenate(
                    [delta_s[2 * pair + side : 2 * pair + side + 1, q_rows] for side in (0, 1)], 1
                )
                scores = dot_nt(kv_s[k_rows, lanes], queries) + bias
                probs = jnp.exp(scores - lse)
                d_probs = dot_nt(kv_s[k_rows, v_lanes], d_out)
                d_scores = (probs * (d_probs - delta)).astype(BF16)
                dkv_s[k_rows, v_lanes] += dot(probs.astype(BF16), d_out)
                dkv_s[k_rows, lanes] += dot(d_scores, queries)
                for side in (0, 1):
                    heads = slice(128 * pair + 64 * side, 128 * pair + 64 * side + 64)
                    part = slice(q_tile * side, q_tile * side + q_tile)
                    dqt_s[heads, :] += dot(kt_s[heads, k_rows], d_scores[:, part])
            return inner

        high = (first + q_at + q_tile - 1) // K_BACK + 1
        lax.fori_loop(low[q_at // Q_TILE] // K_BACK, high, k_step, 0)
        cosine, sine = cos_ref[q_rows, :], sin_ref[q_rows, :]
        for pair in range(HEADS // 2):
            lanes = slice(128 * pair, 128 * pair + 128)
            block = dqt_s[lanes, :].T * HEAD_DIM**-0.5
            dq_ref[q_rows, lanes] = (block * cosine - swap_halves(block) * sine).astype(BF16)
        return carry

    lax.fori_loop(0, tokens // q_tile, q_step, 0)
    for index, ref in enumerate(dkv_refs):
        at = pl.multiple_of(bands[index + 1] * tokens, tokens)
        dlow_s[index] = dkv_s[pl.ds(at, tokens), :].astype(BF16)
        pltpu.make_async_copy(dlow_s.at[index], ref, sem).start()
    wait_whole(dlow_s, sem)


def attend_back(low, bands, queries, d_out, out, lse, mark_row, mark_col, cosine, sine, kv_list, total, ride=(), before=()):
    tokens, width = queries.shape
    n_kv = len(kv_list)
    return call(
        functools.partial(attend_back_kernel, n_kv),
        "attend_back",
        (
            jax.ShapeDtypeStruct((tokens, width), BF16),
            *([jax.ShapeDtypeStruct((tokens, 2 * width), BF16)] * n_kv),
        ),
        [SMEM, SMEM] + [VMEM] * 8 + [ANY] * n_kv,
        (VMEM, *([ANY] * n_kv)),
        [
            pltpu.VMEM((total, 2 * width), BF16),
            pltpu.VMEM((width, total), BF16),
            pltpu.VMEM((width, min(Q_BACK, tokens)), F32),
            pltpu.VMEM((total, 2 * width), F32),
            pltpu.VMEM((n_kv, tokens, 2 * width), BF16),
            pltpu.VMEM((16, tokens), F32),
            pltpu.SemaphoreType.DMA,
        ],
        (low, bands, queries, d_out, out, lse, mark_row, mark_col, cosine, sine, *kv_list),
        20,
        ride,
        before,
    )


def pre_back_kernel(
    n_w,
    n_g,
    n_kv,
    order,
    table,
    x_ref,
    dq_ref,
    cos_ref,
    sin_ref,
    gains_ref,
    dmid_ref,
    ggain_ref,
    att_ref,
    dattn_ref,
    *refs,
):
    dkv_refs, w_refs = refs[:n_kv], refs[n_kv : n_kv + n_w]
    refs = refs[n_kv + n_w :]
    flow_ref, g_refs = refs[0], refs[1 : 1 + n_g]
    w_s, hidt_s, dqkv_s, attt_s, g_s, sem = refs[1 + n_g :]
    tokens, width = x_ref.shape
    start_weights(order, w_refs, w_s, sem)
    gain = gains_ref[0:1, :]
    tile = row_tile(tokens)
    wait_whole(w_s, sem)
    ggain = jnp.zeros((1, width), F32)
    for start in range(0, tokens, tile):
        at = slice(start, start + tile)
        x = x_ref[at, :].astype(F32)
        factor = lax.rsqrt(jnp.mean(x * x, -1, keepdims=True) + EPS)
        normed = x * factor
        hidt_s[:, at] = (normed * gain).T.astype(BF16)
        attt_s[:, at] = att_ref[at, :].astype(F32).T.astype(BF16)
        cosine, sine = cos_ref[at, :], sin_ref[at, :]
        dqkv_s[at, :width] = dq_ref[at, :]
        for col in range(0, 2 * width, 128):
            block = dkv_refs[0][at, col : col + 128].astype(F32)
            for ref in dkv_refs[1:]:
                block = block + ref[at, col : col + 128].astype(F32)
            if col < width:
                block = block * cosine - swap_halves(block) * sine
            dqkv_s[at, width + col : width + col + 128] = block.astype(BF16)
        d_hid = dot_nt(dqkv_s[at, :], w_s[:, : 3 * width])
        ggain = ggain + jnp.sum(d_hid * normed, 0, keepdims=True)
        shaped = d_hid * gain
        flow_ref[at, :] = dmid_ref[at, :] + factor * (
            shaped - normed * jnp.mean(shaped * normed, -1, keepdims=True)
        )
    row = lax.broadcasted_iota(jnp.int32, (128, width), 0)
    both = jnp.where(row == 0, ggain, jnp.where(row == 1, ggain_ref[0:1, :], 0.0))
    g_s[:, 4 * width : 4 * width + 128] = both.T.astype(BF16)
    g_s[:, 4 * width + 128 :] = jnp.zeros((width, 128), BF16)
    g_s[:, 3 * width : 4 * width] = dot(attt_s[...], dattn_ref[...]).astype(BF16)

    def columns(step, carry):
        col = pl.multiple_of(step * 256, 256)
        g_s[:, pl.ds(col, 256)] = dot(hidt_s[...], dqkv_s[:, pl.ds(col, 256)]).astype(BF16)
        return carry

    lax.fori_loop(0, 3 * width // 256, columns, 0)
    send_out(table, g_s, g_refs, sem)
    wait_whole(g_s, sem)


def pre_back(
    order,
    table,
    shapes,
    x,
    dq,
    cosine,
    sine,
    gains,
    d_mid,
    ggain,
    attended,
    d_attn,
    dkv_list,
    weights,
    ride=(),
    before=(),
):
    tokens, width = x.shape
    return call(
        functools.partial(pre_back_kernel, len(weights), len(shapes), len(dkv_list)),
        "pre_back",
        (jax.ShapeDtypeStruct((tokens, width), F32), *shapes),
        [SMEM, SMEM] + [VMEM] * (9 + len(dkv_list)) + [ANY] * len(weights),
        (VMEM, *([ANY] * len(shapes))),
        [
            pltpu.VMEM((width, qkv_cols(width)), BF16),
            pltpu.VMEM((width, tokens), BF16),
            pltpu.VMEM((tokens, 3 * width), BF16),
            pltpu.VMEM((width, tokens), BF16),
            pltpu.VMEM((width, width + qkv_cols(width)), BF16),
            pltpu.SemaphoreType.DMA,
        ],
        (
            order,
            table,
            x,
            dq,
            cosine,
            sine,
            gains,
            d_mid,
            ggain,
            attended,
            d_attn,
            *dkv_list,
            *weights,
        ),
        15,
        ride,
        before,
    )


class Layout:
    def __init__(self, n_rows, n_seq, width, ff):
        self.n_rows, self.n_seq = n_rows, n_seq
        self.paired = n_rows % 2 == 0 and n_seq % 2 == 0
        self.ringed = (
            n_rows % 4 == 0 and (width // n_rows) % 16 == 0 and (ff // n_rows) % 16 == 0
        )

    def device(self, row, seq):
        return row * self.n_seq + seq

    def pairs(self, move):
        return [
            (self.device(row, seq), self.device(*move(row, seq)))
            for row in range(self.n_rows)
            for seq in range(self.n_seq)
        ]

    def send(self, value, move):
        return lax.ppermute(value, BOTH, self.pairs(move))

    def to_core(self, value):
        return self.send(value, lambda row, seq: (row ^ 1, seq))

    def to_y(self, value):
        return self.send(value, lambda row, seq: (row ^ 2, seq))

    def to_z(self, value, hops):
        return self.send(value, lambda row, seq: ((row + 4 * hops) % self.n_rows, seq))

    def to_x(self, value):
        return self.send(value, lambda row, seq: (row, (seq + 1) % self.n_seq))

    def regroup(self, row, seq):
        if not self.paired:
            return (row, seq)
        return (row - row % 2 + seq % 2, (row % 2) * (self.n_seq // 2) + seq // 2)

    def into_groups(self, value):
        return self.send(value, self.regroup) if self.paired else value

    def out_of_groups(self, value):
        if not self.paired:
            return value
        back = [(there, here) for here, there in self.pairs(self.regroup)]
        return lax.ppermute(value, BOTH, back)

    def band(self, row, seq):
        if not self.paired:
            return seq
        return (seq % (self.n_seq // 2)) * 2 + row % 2

    def groups(self):
        places = {}
        for row in range(self.n_rows):
            for seq in range(self.n_seq):
                there = self.regroup(row, seq)
                places.setdefault(row, {})[seq] = self.device(*there)
        return [[places[row][seq] for seq in range(self.n_seq)] for row in range(self.n_rows)]


def on_device(n_rows, n_seq, *args):
    inputs, seg_start, w_q, w_k, w_v, w_o, w_g, w_u, w_d, norm_attn, norm_mlp, cotangent = args
    _, tokens, width = inputs.shape
    ff = w_g.shape[2]
    total = tokens * n_seq
    lay = Layout(n_rows, n_seq, width, ff)
    row_at, seq_at = lax.axis_index("rows"), lax.axis_index("seq")
    ringed = lay.ringed and n_seq == 2
    depth = n_rows // 4

    def bundles(layer):
        gains = jnp.stack([norm_attn[layer], norm_mlp[layer]], 1)
        gains = jnp.pad(gains, ((0, 0), (0, 254)))
        return [
            jnp.concatenate([w_q[layer], w_k[layer], w_v[layer], gains], 1),
            jnp.concatenate([w_o[layer], w_g[layer], w_u[layer]], 1),
            w_d[layer],
        ]

    def split(cols, parts):
        if not ringed:
            return [(0, cols, "offload")]
        found, first = [], 0
        for count, (share, mode) in enumerate(parts, 1):
            size = cols - first if count == len(parts) else round(cols * share / 256) * 256
            found.append((first, size, mode))
            first += size
        return found

    def table(sign, pieces):
        numbers, columns = [], []
        for first, size, mode in pieces:
            if mode == "offload":
                numbers.append(jnp.int32(0))
                columns.append(jnp.int32(first // 128))
                continue
            for core in (0, 1):
                for half in (0, 1) if mode == "half" else (0,):
                    for side in (0, 2):
                        for hop in range(depth):
                            numbers.append(((row_at + sign * 4 * hop) % n_rows) ^ core ^ side)
                            columns.append(
                                first // 128 + (seq_at ^ half) * (size // 256)
                                if mode == "half"
                                else jnp.int32(first // 128)
                            )
        return jnp.stack([jnp.stack(numbers), jnp.stack(columns)]).astype(jnp.int32)

    def shapes(rows, pieces):
        found = []
        for _, size, mode in pieces:
            if mode == "offload":
                found.append(jax.ShapeDtypeStruct((1, rows, size), BF16))
            elif mode == "half":
                found += [jax.ShapeDtypeStruct((2 * depth, rows // n_rows, size // 2), BF16)] * 4
            else:
                found += [jax.ShapeDtypeStruct((depth, rows // n_rows, size), BF16)] * 4
        return found

    def up(value):
        return value.astype(F32)

    class Gather:
        def __init__(self, shard, mode):
            self.mode, self.stacks, self.level = mode, None, 0
            if mode == "offload":
                self.stacks = [lax.all_gather(shard, "rows", axis=0, tiled=True)[None]]
                return
            if mode == "half":
                columns = shard.shape[1] // 2
                shard = lax.dynamic_slice_in_dim(shard, seq_at * columns, columns, 1)
            self.stay, self.flying = [shard], []
            while len(self.flying) + 1 < depth:
                self.flying.append(lay.to_z((self.stay + self.flying)[-1], 1))

        def step(self):
            self.level += 1
            if self.stacks is not None:
                return
            if self.level == 1:
                near = jnp.stack(self.stay + self.flying)
                self.stay, self.flying = [near], [lay.to_y(near)]
            elif self.level == 2 and self.mode == "whole":
                near, far = self.stay[0], self.flying[0]
                self.stacks = [near, far, lay.to_core(near), lay.to_core(far)]
            elif self.level == 2:
                both = jnp.concatenate([self.stay[0], self.flying[0]])
                self.stay, self.flying = [both], [lay.to_x(both)]
            else:
                both, other = self.stay[0], self.flying[0]
                self.stacks = [both, other, lay.to_core(both), lay.to_core(other)]

        def finish(self):
            while self.stacks is None:
                self.step()
            return self.stacks

    class Scatter:
        def __init__(self, stack, mode):
            self.mode, self.sum, self.level, self.old = mode, None, 0, False
            if mode == "offload":
                summed = lax.psum_scatter(stack[0][0], "rows", scatter_dimension=0, tiled=True)
                if n_seq == 2:
                    self.stay, self.flying, self.level = [summed], [lay.to_x(summed)], 9
                else:
                    self.sum = up(lax.psum(summed, "seq"))
                return
            self.flying = [lay.to_core(stack[3]), lay.to_core(stack[2])]
            self.stay = [stack[1], stack[0]]

        def along_z(self, both):
            sent = [both[hop].astype(BF16) for hop in range(1, depth)]
            self.flying = [lay.to_z(value, hop) for hop, value in enumerate(sent, 1)]
            self.stay = [both[0]]
            return sent

        def step(self):
            if self.sum is not None:
                return []
            self.level += 1
            half = self.mode == "half"
            stay, flying = self.stay, self.flying
            if self.level == 1:
                first = (up(stay[0]) + up(flying[0])).astype(BF16)
                self.stay = [stay[1]]
                self.flying = [lay.to_x(first) if half else lay.to_y(first), flying[1]]
                return [first]
            if self.level == 2:
                both = up(stay[0]) + up(flying[1]) + up(flying[0])
                if not half:
                    return self.along_z(both)
                far = both[depth:].astype(BF16)
                self.stay, self.flying = [both[:depth]], [lay.to_y(far)]
                return [far]
            if self.level == 3 and half:
                return self.along_z(stay[0] + up(flying[0]))
            if self.level == (4 if half else 3):
                total = up(stay[0])
                for value in flying:
                    total = total + up(value)
                total = total.astype(BF16)
                self.stay, self.flying = [total], [lay.to_x(total)]
                return [total]
            mine, other = stay[0], flying[0]
            if not half:
                self.sum = up(mine) + up(other)
                return []
            self.sum = up(
                jnp.where(
                    seq_at == 0,
                    jnp.concatenate([mine, other], 1),
                    jnp.concatenate([other, mine], 1),
                )
            )
            return []

        def finish(self):
            while self.sum is None:
                self.step()
            return self.sum

    def scatters(arrays, pieces):
        found, at = [], 0
        for _, _, mode in pieces:
            size = 1 if mode == "offload" else 4
            found.append(Scatter(arrays[at : at + size], mode))
            at += size
        return found

    def joined(chains):
        sums = [chain.finish() for chain in chains]
        return sums[0] if len(sums) == 1 else jnp.concatenate(sums, 1)

    x_in = lay.into_groups(inputs[0])
    starts_mine = lay.into_groups(seg_start[0])
    d_top = lay.into_groups(cotangent[0])
    groups = lay.groups()
    half_seq = n_seq // 2
    band = (seq_at % half_seq) * 2 + row_at % 2 if lay.paired else seq_at
    two = lay.paired and n_seq == 2

    def exchange(value):
        if two:
            return [value, lay.to_core(value)]
        whole = lax.all_gather(value, BOTH, axis=0, axis_index_groups=groups)
        return [whole[index] for index in range(n_seq)]

    if two:
        bands = jnp.stack([band, band, 1 - band]).astype(jnp.int32)
    else:
        bands = jnp.concatenate([band[None], jnp.arange(n_seq)]).astype(jnp.int32)

    index = band * tokens + jnp.arange(tokens, dtype=jnp.int32)
    positions = jnp.where(starts_mine >= 0, index - starts_mine, 0)
    inverse = THETA ** (-jnp.arange(HEAD_DIM // 2, dtype=F32) * 2.0 / HEAD_DIM)
    angles = positions.astype(F32)[:, None] * inverse
    cosine = jnp.tile(jnp.cos(angles), (1, 4))
    sine = jnp.sin(angles)
    sine = jnp.concatenate([-sine, sine, -sine, sine], 1)
    marks = jnp.where(starts_mine >= 0, starts_mine, -1 - index)
    mark_row = jnp.broadcast_to(marks[None, :], (8, tokens))
    pieces = exchange(marks)
    if two:
        marks_all = jnp.where(
            band == 0, jnp.concatenate(pieces), jnp.concatenate([pieces[1], pieces[0]])
        )
    else:
        marks_all = jnp.concatenate(pieces)
    mark_col = jnp.broadcast_to(marks_all[:, None], (total, 128))
    reach = jnp.where(starts_mine >= 0, starts_mine, index)
    low = jnp.min(reach.reshape(-1, Q_TILE), 1).astype(jnp.int32)

    in_widths = (qkv_cols(width), width + 2 * ff, width)
    out_widths = (width + qkv_cols(width), 2 * ff, width)
    in_pieces = [[split(c, p) for c, p in zip(in_widths, parts)] for parts in IN_PARTS]
    out_pieces = [[split(c, p) for c, p in zip(out_widths, parts)] for parts in OUT_PARTS]
    known = {}

    def table_of(sign, pieces):
        key = (sign, *pieces)
        if key not in known:
            known[key] = table(sign, pieces)
        return known[key]

    orders = [[table_of(-1, pieces) for pieces in in_pieces[layer]] for layer in range(LAYERS)]
    tables = [[table_of(1, pieces) for pieces in out_pieces[layer]] for layer in range(LAYERS)]

    def gathers(shard, pieces):
        return [Gather(shard[:, first : first + size], mode) for first, size, mode in pieces]

    def arrived(chains):
        return [stack for chain in chains for stack in chain.finish()]

    kept = []
    current = x_in
    weights = []

    def near_of(bundles_of_chains):
        found = []
        for chains_here in bundles_of_chains:
            for chain in chains_here:
                if chain.stacks is None:
                    chain.step()
                    found += chain.stay
        return found

    shards = bundles(0)
    moving = [[gathers(shards[0], in_pieces[0][0])], None]
    if ringed:
        _ = ([value for chain in moving[0][0] for value in chain.flying], shards[1:])
    moving[0] += [gathers(s, p) for s, p in zip(shards[1:], in_pieces[0][1:])]
    for layer in range(LAYERS):
        last = layer + 1 == LAYERS
        o_qkv, o_ogu, o_down = orders[layer]
        w_qkv = arrived(moving[layer][0])
        (queries, kv, gains), ridden = pre(
            o_qkv,
            current,
            cosine,
            sine,
            w_qkv,
            ride=[] if last else bundles(layer + 1),
        )
        kv_list = exchange(kv)
        (attended, lse), _ = attend(
            low,
            bands,
            queries,
            mark_row,
            mark_col,
            kv_list,
            total,
        )
        before = []
        if not last:
            moving[layer + 1] = [gathers(s, p) for s, p in zip(ridden, in_pieces[layer + 1])]
        w_ogu, w_down = arrived(moving[layer][1]), arrived(moving[layer][2])
        (result, mid, gu), _ = post(
            o_ogu, o_down, ff, current, attended, gains, w_ogu, w_down, before=before
        )
        kept.append((current, queries, kv_list, attended, lse, mid, gu, gains))
        weights.append((w_qkv, w_ogu, w_down))
        current = result
    output = lay.out_of_groups(current.astype(BF16)).astype(F32)

    flow = d_top
    chains = [None] * LAYERS
    live = []

    def through(kernel, *args, **more):
        if not ringed:
            return kernel(*args, **more)[0]
        sent = more.pop("before", [])
        for chain in live:
            if chain.level < 9:
                sent = sent + (chain.step() if chain.old else [])
            chain.old = True
        holders = [chain for chain in live if chain.sum is None and chain.level < 9]
        ride = [value for chain in holders for value in chain.stay]
        results, ridden = kernel(*args, ride=ride, before=sent, **more)
        for chain in holders:
            chain.stay, ridden = ridden[: len(chain.stay)], ridden[len(chain.stay) :]
        return results

    for layer in reversed(range(LAYERS)):
        x, queries, kv_list, attended, lse, mid, gu, gains = kept[layer]
        o_qkv, o_ogu, o_down = orders[layer]
        w_qkv, w_ogu, w_down = weights[layer]
        t_qkv, t_gu, t_down = tables[layer]
        p_qkv, p_gu, p_down = out_pieces[layer]
        s_gu, s_down = shapes(width, p_gu), shapes(ff, p_down)
        results = through(
            mlp_back, o_down, (t_gu, t_down), (s_gu, s_down), flow, mid, gu, gains, w_down
        )
        dgu = results[0]
        c_gu = scatters(results[1 : 1 + len(s_gu)], p_gu)
        c_down = scatters(results[1 + len(s_gu) :], p_down)
        live += c_gu + c_down
        d_mid, d_attn, d_att, ggain = through(mid_back, o_ogu, flow, mid, dgu, gains, w_ogu)
        results = through(
            attend_back,
            low,
            bands,
            queries,
            d_att,
            attended,
            lse,
            mark_row,
            mark_col,
            cosine,
            sine,
            kv_list,
            total,
        )
        dq, dkv = results[0], results[1:]
        if two:
            dkv_list = [dkv[0], lay.to_core(dkv[1])]
        else:
            dkv_list = [
                lax.psum_scatter(
                    jnp.stack(dkv), BOTH, scatter_dimension=0, axis_index_groups=groups
                )
            ]
        s_qkv = shapes(width, p_qkv)
        results = through(
            pre_back,
            o_qkv,
            t_qkv,
            s_qkv,
            x,
            dq,
            cosine,
            sine,
            gains,
            d_mid,
            ggain,
            attended,
            d_attn,
            dkv_list,
            w_qkv,
            before=[output] if layer == 0 else [],
        )
        flow = results[0]
        c_qkv = scatters(results[1:], p_qkv)
        live += c_qkv
        chains[layer] = (c_qkv, c_gu, c_down)
    while ringed and any(chain.sum is None and chain.level < 9 for chain in live):
        through(lambda ride, before: ([], gate(before, ride)))
    grads = [[joined(part) for part in chains[layer]] for layer in range(LAYERS)]
    grad_input = lay.out_of_groups(flow.astype(BF16)).astype(F32)

    def stack(which, first, size):
        return jnp.stack([grads[layer][which][:, first : first + size] for layer in range(LAYERS)])

    return (
        output[None],
        grad_input[None],
        stack(0, 0, width),
        stack(0, width, width),
        stack(0, 2 * width, width),
        stack(0, 3 * width, width),
        stack(1, 0, ff),
        stack(1, ff, ff),
        stack(2, 0, width),
        stack(0, 4 * width, 1)[..., 0],
        stack(0, 4 * width + 1, 1)[..., 0],
    )


def solution(mesh):
    rows3, rows2 = P("rows", "seq", None), P("rows", "seq")
    weight, vector = P(None, "rows", None), P(None, "rows")
    return jax.shard_map(
        functools.partial(on_device, mesh.shape["rows"], mesh.shape["seq"]),
        mesh=mesh,
        in_specs=(rows3, rows2, *([weight] * 7), vector, vector, rows3),
        out_specs=(rows3, rows3, *([weight] * 7), vector, vector),
        check_vma=False,
    )
```

```python
import functools

import jax
import jax.numpy as jnp
from jax import lax
from jax.experimental import pallas as pl
from jax.experimental.pallas import tpu as pltpu
from jax.sharding import PartitionSpec as P

HEADS = 12
HEAD_DIM = 64
LAYERS = 2
EPS = 1e-05
NEG_BIG = -1e30
THETA = 10000.0
F32 = jnp.float32
BF16 = jnp.bfloat16
BOTH = ("rows", "seq")
SMEM = pl.BlockSpec(memory_space=pltpu.SMEM)
VMEM = pl.BlockSpec(memory_space=pltpu.VMEM)
ANY = pl.BlockSpec(memory_space=pl.ANY)
VMEM_MIB = dict(
    gate=2, pre=18, attend=14, post=32, mlp_back=38, mid_back=28, attend_back=28, pre_back=34
)
Q_TILE, K_TILE = 128, 128
Q_BACK, K_BACK = 256, 256
FLOPS_PER_US = 1.1e9
IN_PARTS = (
    ([(1.0, "whole")], [(0.5, "whole"), (0.5, "half")], [(1.0, "half")]),
    ([(1.0, "half")], [(1.0, "whole")], [(1.0, "half")]),
)
OUT_PARTS = (
    ([(0.5, "whole"), (0.5, "half")], [(1.0, "offload")], [(1.0, "half")]),
    ([(1.0, "half")], [(1.0, "offload")], [(1.0, "half")]),
)


def dot(left, right):
    return jnp.dot(left, right, preferred_element_type=F32)


def dot_nt(left, right):
    return lax.dot_general(left, right, (((1,), (1,)), ((), ())), preferred_element_type=F32)


def swap_halves(block):
    lane = lax.broadcasted_iota(jnp.int32, block.shape, 1)
    return jnp.where(lane % 64 < 32, pltpu.roll(block, 96, 1), pltpu.roll(block, 32, 1))


def place(table, index, rows, cols, whole):
    at = pl.ds(pl.multiple_of(table[0, index] * rows, 16), rows)
    if cols == whole.shape[1]:
        return whole.at[at, :]
    return whole.at[at, pl.ds(pl.multiple_of(table[1, index] * 128, 128), cols)]


def start_weights(table, refs, held, sem):
    index = 0
    for ref in refs:
        for part in range(ref.shape[0]):
            target = place(table, index, ref.shape[1], ref.shape[2], held)
            pltpu.make_async_copy(ref.at[part], target, sem).start()
            index += 1


def wait_whole(held, sem):
    pltpu.make_async_copy(held, held, sem).wait()


def send_out(table, whole, refs, sem):
    index = 0
    for ref in refs:
        for part in range(ref.shape[0]):
            source = place(table, index, ref.shape[1], ref.shape[2], whole)
            pltpu.make_async_copy(source, ref.at[part], sem).start()
            index += 1


def call(kernel, name, out_shape, in_specs, out_specs, scratch, args, micros, ride=(), before=()):
    n_in, n_out, n_ride = len(in_specs), len(out_specs), len(ride)
    n_more = n_ride + len(before)

    def wrapped(*refs):
        outs_at = n_in + n_more
        kernel(*refs[:n_in], *refs[outs_at : outs_at + n_out], *refs[outs_at + n_out + n_ride :])

    results = pl.pallas_call(
        wrapped,
        name=name,
        out_shape=(*out_shape, *(jax.ShapeDtypeStruct(a.shape, a.dtype) for a in ride)),
        in_specs=[*in_specs, *([ANY] * n_more)],
        out_specs=(*out_specs, *([ANY] * n_ride)),
        scratch_shapes=scratch,
        input_output_aliases={n_in + i: n_out + i for i in range(n_ride)},
        compiler_params=pltpu.CompilerParams(vmem_limit_bytes=VMEM_MIB[name] * 1024 * 1024),
        cost_estimate=pl.CostEstimate(
            flops=int(micros * FLOPS_PER_US), bytes_accessed=0, transcendentals=0
        ),
    )(*args, *ride, *before)
    return results[:n_out], list(results[n_out:])


def qkv_cols(width):
    return 3 * width + 256


def row_tile(tokens):
    return min(256, tokens)


def pre_kernel(n_w, order, x_ref, cos_ref, sin_ref, *refs):
    w_refs = refs[:n_w]
    q_ref, kv_ref, gains_ref, w_s, hid_s, sem = refs[n_w:]
    tokens, width = x_ref.shape
    start_weights(order, w_refs, w_s, sem)
    wait_whole(w_s, sem)
    gains_ref[...] = w_s[:, 3 * width : 3 * width + 128].astype(F32).T[:8]
    gain = gains_ref[0:1, :]
    tile = row_tile(tokens)

    def body(step, carry):
        at = pl.ds(pl.multiple_of(step * tile, tile), tile)
        x = x_ref[at, :].astype(F32)
        factor = lax.rsqrt(jnp.mean(x * x, -1, keepdims=True) + EPS)
        hidden = (x * factor * gain).astype(BF16)
        cosine, sine = cos_ref[at, :], sin_ref[at, :]
        for col in range(0, 3 * width, 256):
            part = dot(hidden, w_s[:, col : col + 256])
            if col < 2 * width:
                halves = []
                for lane in (0, 128):
                    block = part[:, lane : lane + 128]
                    halves.append(block * cosine + swap_halves(block) * sine)
                part = jnp.concatenate(halves, 1)
            if col < width:
                q_ref[at, col : col + 256] = (part * HEAD_DIM**-0.5).astype(BF16)
            else:
                kv_ref[at, col - width : col - width + 256] = part.astype(BF16)
        return carry

    lax.fori_loop(0, tokens // tile, body, 0)


def pre(order, x, cosine, sine, weights, ride=(), before=()):
    tokens, width = x.shape
    cols = qkv_cols(width)
    return call(
        functools.partial(pre_kernel, len(weights)),
        "pre",
        (
            jax.ShapeDtypeStruct((tokens, width), BF16),
            jax.ShapeDtypeStruct((tokens, 2 * width), BF16),
            jax.ShapeDtypeStruct((8, width), F32),
        ),
        [SMEM, VMEM, VMEM, VMEM] + [ANY] * len(weights),
        (VMEM, VMEM, VMEM),
        [
            pltpu.VMEM((width, cols), BF16),
            pltpu.VMEM((tokens, width), BF16),
            pltpu.SemaphoreType.DMA,
        ],
        (order, x, cosine, sine, *weights),
        7,
        ride,
        before,
    )


def gate_kernel(done_ref):
    done_ref[...] = jnp.zeros_like(done_ref)


def gate(before, ride):
    return call(
        gate_kernel, "gate", (jax.ShapeDtypeStruct((8, 128), F32),), [], (VMEM,), [], (), 0, ride, before
    )[1]


def load_bands(bands, kv_refs, kv_s, sem):
    tokens = kv_refs[0].shape[0]
    for index, ref in enumerate(kv_refs):
        at = pl.multiple_of(bands[index + 1] * tokens, tokens)
        pltpu.make_async_copy(ref, kv_s.at[pl.ds(at, tokens), :], sem).start()


def bias_tile(mark_col, mark_row, k_at, q_at, k_tile, q_tile):
    key = k_at + lax.broadcasted_iota(jnp.int32, (k_tile, q_tile), 0)
    query = q_at + lax.broadcasted_iota(jnp.int32, (k_tile, q_tile), 1)
    return jnp.where((mark_col == mark_row) & (key <= query), 0.0, NEG_BIG)


def head_pair(block):
    lane = lax.broadcasted_iota(jnp.int32, block.shape, 1)
    zero = jnp.zeros_like(block)
    return jnp.concatenate(
        [jnp.where(lane < 64, block, zero), jnp.where(lane >= 64, block, zero)], 0
    )


def transpose_tiles(dest, source, first, columns, low, high, k_tile):
    def body(tile, carry):
        at = pl.ds(pl.multiple_of(tile * k_tile, k_tile), k_tile)
        for col in range(0, columns, 128):
            block = source[at, first + col : first + col + 128]
            dest[col : col + 128, at] = block.astype(F32).T.astype(BF16)
        return carry

    lax.fori_loop(low, high, body, 0)


def attend_kernel(n_kv, low, bands, q_ref, row_ref, col_ref, *refs):
    kv_refs = refs[:n_kv]
    out_ref, lse_ref, kv_s, vt_s, acc_s, max_s, sum_s, sem = refs[n_kv:]
    tokens, width = q_ref.shape
    total = kv_s.shape[0]
    load_bands(bands, kv_refs, kv_s, sem)
    wait_whole(kv_s, sem)
    first = bands[0] * tokens
    transpose_tiles(vt_s, kv_s, width, width, low[0] // K_TILE, (first + tokens - 1) // K_TILE + 1, K_TILE)
    lse_ref[...] = jnp.zeros_like(lse_ref)

    def q_step(q_index, carry):
        q_at = pl.multiple_of(q_index * Q_TILE, Q_TILE)
        max_s[...] = jnp.full_like(max_s, NEG_BIG)
        sum_s[...] = jnp.zeros_like(sum_s)
        acc_s[...] = jnp.zeros_like(acc_s)
        mark_row = row_ref[0:1, pl.ds(q_at, Q_TILE)]

        def k_step(k_index, inner):
            k_at = pl.multiple_of(k_index * K_TILE, K_TILE)
            bias = bias_tile(
                col_ref[pl.ds(k_at, K_TILE), :], mark_row, k_at, first + q_at, K_TILE, Q_TILE
            )
            bias = jnp.concatenate([bias, bias], 1)
            for pair in range(HEADS // 2):
                lanes = slice(128 * pair, 128 * pair + 128)
                queries = head_pair(q_ref[pl.ds(q_at, Q_TILE), lanes])
                scores = dot_nt(kv_s[pl.ds(k_at, K_TILE), lanes], queries) + bias
                before = max_s[pair : pair + 1, :]
                highest = jnp.maximum(before, jnp.max(scores, 0, keepdims=True))
                shrink = jnp.exp(before - highest)
                expd = jnp.exp(scores - highest)
                max_s[pair : pair + 1, :] = highest
                sum_s[pair : pair + 1, :] = sum_s[pair : pair + 1, :] * shrink + jnp.sum(
                    expd, 0, keepdims=True
                )
                low_p = expd.astype(BF16)
                for side in (0, 1):
                    heads = slice(128 * pair + 64 * side, 128 * pair + 64 * side + 64)
                    part = slice(Q_TILE * side, Q_TILE * side + Q_TILE)
                    mixed = dot(vt_s[heads, pl.ds(k_at, K_TILE)], low_p[:, part])
                    acc_s[heads, :] = acc_s[heads, :] * shrink[:, part] + mixed
            return inner

        high = (first + q_at + Q_TILE - 1) // K_TILE + 1
        lax.fori_loop(low[q_index] // K_TILE, high, k_step, 0)
        for pair in range(HEADS // 2):
            lanes = slice(128 * pair, 128 * pair + 128)
            scale = 1.0 / sum_s[pair : pair + 1, :]
            lse = max_s[pair : pair + 1, :] + jnp.log(sum_s[pair : pair + 1, :])
            both = []
            for side in (0, 1):
                heads = slice(128 * pair + 64 * side, 128 * pair + 64 * side + 64)
                part = slice(Q_TILE * side, Q_TILE * side + Q_TILE)
                both.append(acc_s[heads, :] * scale[:, part])
                row = 2 * pair + side
                lse_ref[row : row + 1, pl.ds(q_at, Q_TILE)] = lse[:, part]
            out_ref[pl.ds(q_at, Q_TILE), lanes] = jnp.concatenate(both, 0).T.astype(BF16)
        return carry

    lax.fori_loop(0, tokens // Q_TILE, q_step, 0)


def attend(low, bands, queries, mark_row, mark_col, kv_list, total, ride=(), before=()):
    tokens, width = queries.shape
    return call(
        functools.partial(attend_kernel, len(kv_list)),
        "attend",
        (
            jax.ShapeDtypeStruct((tokens, width), BF16),
            jax.ShapeDtypeStruct((16, tokens), F32),
        ),
        [SMEM, SMEM, VMEM, VMEM, VMEM] + [ANY] * len(kv_list),
        (VMEM, VMEM),
        [
            pltpu.VMEM((total, 2 * width), BF16),
            pltpu.VMEM((width, total), BF16),
            pltpu.VMEM((width, Q_TILE), F32),
            pltpu.VMEM((8, 2 * Q_TILE), F32),
            pltpu.VMEM((8, 2 * Q_TILE), F32),
            pltpu.SemaphoreType.DMA,
        ],
        (low, bands, queries, mark_row, mark_col, *kv_list),
        15,
        ride,
        before,
    )


def post_kernel(n_a, n_d, order_a, order_d, x_ref, att_ref, gains_ref, *refs):
    a_refs, d_refs = refs[:n_a], refs[n_a : n_a + n_d]
    out_ref, mid_ref, gu_ref, a_s, d_s, act_s, sem_a, sem_d = refs[n_a + n_d :]
    tokens, width = x_ref.shape
    ff = d_s.shape[0]
    start_weights(order_a, a_refs, a_s, sem_a)
    start_weights(order_d, d_refs, d_s, sem_d)
    wait_whole(a_s, sem_a)
    wait_whole(d_s, sem_d)
    gain = gains_ref[1:2, :]
    tile = row_tile(tokens)

    def body(step, carry):
        at = pl.ds(pl.multiple_of(step * tile, tile), tile)
        mid = x_ref[at, :].astype(F32) + dot(att_ref[at, :], a_s[:, :width])
        mid_ref[at, :] = mid
        factor = lax.rsqrt(jnp.mean(mid * mid, -1, keepdims=True) + EPS)
        hidden = (mid * factor * gain).astype(BF16)
        for col in range(0, ff, 256):
            gate = dot(hidden, a_s[:, width + col : width + col + 256])
            up = dot(hidden, a_s[:, width + ff + col : width + ff + col + 256])
            gu_ref[at, col : col + 256] = gate.astype(BF16)
            gu_ref[at, ff + col : ff + col + 256] = up.astype(BF16)
            act_s[:, col : col + 256] = (gate * jax.nn.sigmoid(gate) * up).astype(BF16)
        out_ref[at, :] = mid + dot(act_s[...], d_s[...])
        return carry

    lax.fori_loop(0, tokens // tile, body, 0)


def post(order_a, order_d, ff, x, attended, gains, w_a, w_d, ride=(), before=()):
    tokens, width = x.shape
    cols = width + 2 * ff
    return call(
        functools.partial(post_kernel, len(w_a), len(w_d)),
        "post",
        (
            jax.ShapeDtypeStruct((tokens, width), F32),
            jax.ShapeDtypeStruct((tokens, width), F32),
            jax.ShapeDtypeStruct((tokens, 2 * ff), BF16),
        ),
        [SMEM, SMEM, VMEM, VMEM, VMEM] + [ANY] * (len(w_a) + len(w_d)),
        (VMEM, VMEM, VMEM),
        [
            pltpu.VMEM((width, cols), BF16),
            pltpu.VMEM((ff, width), BF16),
            pltpu.VMEM((row_tile(tokens), ff), BF16),
            pltpu.SemaphoreType.DMA,
            pltpu.SemaphoreType.DMA,
        ],
        (order_a, order_d, x, attended, gains, *w_a, *w_d),
        14,
        ride,
        before,
    )


def mlp_back_kernel(
    counts, order_d, table_a, table_d, flow_ref, mid_ref, gu_ref, gains_ref, *refs
):
    n_d, n_ga, n_gd = counts
    d_refs, refs = refs[:n_d], refs[n_d:]
    dgu_ref, ga_refs, gd_refs = refs[0], refs[1 : 1 + n_ga], refs[1 + n_ga : 1 + n_ga + n_gd]
    d_s, actt_s, db_s, hidt_s, ga_s, gd_s, sem_a, sem_d = refs[1 + n_ga + n_gd :]
    tokens, width = mid_ref.shape
    ff = d_s.shape[0]
    start_weights(order_d, d_refs, d_s, sem_d)
    gain = gains_ref[1:2, :]
    tile = row_tile(tokens)
    for start in range(0, tokens, tile):
        at = slice(start, start + tile)
        db_s[at, :] = flow_ref[at, :].astype(BF16)
        mid = mid_ref[at, :]
        factor = lax.rsqrt(jnp.mean(mid * mid, -1, keepdims=True) + EPS)
        hidt_s[:, at] = (mid * factor * gain).T.astype(BF16)
    wait_whole(d_s, sem_d)

    def columns(step, carry):
        col = pl.multiple_of(step * 256, 256)
        for start in range(0, tokens, tile):
            at = slice(start, start + tile)
            d_act = dot_nt(db_s[at, :], d_s[pl.ds(col, 256), :])
            gate = gu_ref[at, pl.ds(col, 256)].astype(F32)
            up = gu_ref[at, pl.ds(ff + col, 256)].astype(F32)
            sigma = jax.nn.sigmoid(gate)
            silu = gate * sigma
            actt_s[pl.ds(col, 256), at] = (silu * up).T.astype(BF16)
            dgu_ref[at, pl.ds(col, 256)] = (
                d_act * up * (sigma * (1.0 + gate * (1.0 - sigma)))
            ).astype(BF16)
            dgu_ref[at, pl.ds(ff + col, 256)] = (d_act * silu).astype(BF16)
        for first in (0, ff):
            ga_s[:, pl.ds(first + col, 256)] = dot(
                hidt_s[...], dgu_ref[:, pl.ds(first + col, 256)]
            ).astype(BF16)
        rows = pl.ds(col, 256)
        gd_s[rows, :] = dot(actt_s[rows, :], db_s[...]).astype(BF16)
        return carry

    lax.fori_loop(0, ff // 256, columns, 0)
    send_out(table_a, ga_s, ga_refs, sem_a)
    send_out(table_d, gd_s, gd_refs, sem_d)
    wait_whole(ga_s, sem_a)
    wait_whole(gd_s, sem_d)


def mlp_back(order_d, tables, shapes, flow, mid, gu, gains, w_d, ride=(), before=()):
    tokens, width = mid.shape
    ff = gu.shape[1] // 2
    ga, gd = shapes
    return call(
        functools.partial(mlp_back_kernel, (len(w_d), len(ga), len(gd))),
        "mlp_back",
        (jax.ShapeDtypeStruct((tokens, 2 * ff), BF16), *ga, *gd),
        [SMEM] * 3 + [VMEM] * 4 + [ANY] * len(w_d),
        (VMEM, *([ANY] * (len(ga) + len(gd)))),
        [
            pltpu.VMEM((ff, width), BF16),
            pltpu.VMEM((ff, tokens), BF16),
            pltpu.VMEM((tokens, width), BF16),
            pltpu.VMEM((width, tokens), BF16),
            pltpu.VMEM((width, 2 * ff), BF16),
            pltpu.VMEM((ff, width), BF16),
            pltpu.SemaphoreType.DMA,
            pltpu.SemaphoreType.DMA,
        ],
        (order_d, *tables, flow, mid, gu, gains, *w_d),
        20,
        ride,
        before,
    )


def mid_back_kernel(n_a, order_a, flow_ref, mid_ref, dgu_ref, gains_ref, *refs):
    a_refs = refs[:n_a]
    dmid_ref, dattn_ref, datt_ref, ggain_ref, a_s, sem = refs[n_a:]
    tokens, width = mid_ref.shape
    start_weights(order_a, a_refs, a_s, sem)
    gain = gains_ref[1:2, :]
    tile = row_tile(tokens)
    wait_whole(a_s, sem)
    ggain = jnp.zeros((1, width), F32)
    for start in range(0, tokens, tile):
        at = slice(start, start + tile)
        mid = mid_ref[at, :]
        factor = lax.rsqrt(jnp.mean(mid * mid, -1, keepdims=True) + EPS)
        normed = mid * factor
        d_hid = dot_nt(dgu_ref[at, :], a_s[:, width:])
        ggain = ggain + jnp.sum(d_hid * normed, 0, keepdims=True)
        shaped = d_hid * gain
        d_mid = flow_ref[at, :].astype(F32) + factor * (
            shaped - normed * jnp.mean(shaped * normed, -1, keepdims=True)
        )
        dmid_ref[at, :] = d_mid
        d_attn = d_mid.astype(BF16)
        dattn_ref[at, :] = d_attn
        datt_ref[at, :] = dot_nt(d_attn, a_s[:, :width]).astype(BF16)
    ggain_ref[...] = jnp.broadcast_to(ggain, ggain_ref.shape)


def mid_back(order_a, flow, mid, dgu, gains, w_a, ride=(), before=()):
    tokens, width = mid.shape
    return call(
        functools.partial(mid_back_kernel, len(w_a)),
        "mid_back",
        (
            jax.ShapeDtypeStruct((tokens, width), F32),
            jax.ShapeDtypeStruct((tokens, width), BF16),
            jax.ShapeDtypeStruct((tokens, width), BF16),
            jax.ShapeDtypeStruct((8, width), F32),
        ),
        [SMEM] + [VMEM] * 4 + [ANY] * len(w_a),
        (VMEM, VMEM, VMEM, VMEM),
        [
            pltpu.VMEM((width, width + dgu.shape[1]), BF16),
            pltpu.SemaphoreType.DMA,
        ],
        (order_a, flow, mid, dgu, gains, *w_a),
        13,
        ride,
        before,
    )


def attend_back_kernel(
    n_kv, low, bands, q_ref, do_ref, out_ref, lse_ref, row_ref, col_ref, cos_ref, sin_ref, *refs
):
    kv_refs = refs[:n_kv]
    dq_ref = refs[n_kv]
    dkv_refs = refs[n_kv + 1 : 2 * n_kv + 1]
    kv_s, kt_s, dqt_s, dkv_s, dlow_s, delta_s, sem = refs[2 * n_kv + 1 :]
    tokens, width = q_ref.shape
    q_tile = min(Q_BACK, tokens)
    total = kv_s.shape[0]
    load_bands(bands, kv_refs, kv_s, sem)
    head_of = lax.broadcasted_iota(jnp.int32, (16, width), 1) // HEAD_DIM
    picks = (head_of == lax.broadcasted_iota(jnp.int32, (16, width), 0)).astype(BF16)
    product = do_ref[...].astype(F32) * out_ref[...].astype(F32)
    upper = product.astype(BF16)
    lower = (product - upper.astype(F32)).astype(BF16)
    delta_s[...] = dot_nt(picks, upper) + dot_nt(picks, lower)
    dkv_s[...] = jnp.zeros_like(dkv_s)
    wait_whole(kv_s, sem)
    first = bands[0] * tokens
    transpose_tiles(kt_s, kv_s, 0, width, low[0] // K_BACK, (first + tokens - 1) // K_BACK + 1, K_BACK)

    def q_step(q_index, carry):
        q_at = pl.multiple_of(q_index * q_tile, q_tile)
        q_rows = pl.ds(q_at, q_tile)
        dqt_s[...] = jnp.zeros_like(dqt_s)
        mark_row = row_ref[0:1, q_rows]

        def k_step(k_index, inner):
            k_at = pl.multiple_of(k_index * K_BACK, K_BACK)
            k_rows = pl.ds(k_at, K_BACK)
            bias = bias_tile(col_ref[k_rows, 0:1], mark_row, k_at, first + q_at, K_BACK, q_tile)
            bias = jnp.concatenate([bias, bias], 1)
            for pair in range(HEADS // 2):
                lanes = slice(128 * pair, 128 * pair + 128)
                v_lanes = slice(width + 128 * pair, width + 128 * pair + 128)
                queries = head_pair(q_ref[q_rows, lanes])
                d_out = head_pair(do_ref[q_rows, lanes])
                lse = jnp.concatenate(
                    [lse_ref[2 * pair + side : 2 * pair + side + 1, q_rows] for side in (0, 1)], 1
                )
                delta = jnp.concatenate(
                    [delta_s[2 * pair + side : 2 * pair + side + 1, q_rows] for side in (0, 1)], 1
                )
                scores = dot_nt(kv_s[k_rows, lanes], queries) + bias
                probs = jnp.exp(scores - lse)
                d_probs = dot_nt(kv_s[k_rows, v_lanes], d_out)
                d_scores = (probs * (d_probs - delta)).astype(BF16)
                dkv_s[k_rows, v_lanes] += dot(probs.astype(BF16), d_out)
                dkv_s[k_rows, lanes] += dot(d_scores, queries)
                for side in (0, 1):
                    heads = slice(128 * pair + 64 * side, 128 * pair + 64 * side + 64)
                    part = slice(q_tile * side, q_tile * side + q_tile)
                    dqt_s[heads, :] += dot(kt_s[heads, k_rows], d_scores[:, part])
            return inner

        high = (first + q_at + q_tile - 1) // K_BACK + 1
        lax.fori_loop(low[q_at // Q_TILE] // K_BACK, high, k_step, 0)
        cosine, sine = cos_ref[q_rows, :], sin_ref[q_rows, :]
        for pair in range(HEADS // 2):
            lanes = slice(128 * pair, 128 * pair + 128)
            block = dqt_s[lanes, :].T * HEAD_DIM**-0.5
            dq_ref[q_rows, lanes] = (block * cosine - swap_halves(block) * sine).astype(BF16)
        return carry

    lax.fori_loop(0, tokens // q_tile, q_step, 0)
    for index, ref in enumerate(dkv_refs):
        at = pl.multiple_of(bands[index + 1] * tokens, tokens)
        dlow_s[index] = dkv_s[pl.ds(at, tokens), :].astype(BF16)
        pltpu.make_async_copy(dlow_s.at[index], ref, sem).start()
    wait_whole(dlow_s, sem)


def attend_back(low, bands, queries, d_out, out, lse, mark_row, mark_col, cosine, sine, kv_list, total, ride=(), before=()):
    tokens, width = queries.shape
    n_kv = len(kv_list)
    return call(
        functools.partial(attend_back_kernel, n_kv),
        "attend_back",
        (
            jax.ShapeDtypeStruct((tokens, width), BF16),
            *([jax.ShapeDtypeStruct((tokens, 2 * width), BF16)] * n_kv),
        ),
        [SMEM, SMEM] + [VMEM] * 8 + [ANY] * n_kv,
        (VMEM, *([ANY] * n_kv)),
        [
            pltpu.VMEM((total, 2 * width), BF16),
            pltpu.VMEM((width, total), BF16),
            pltpu.VMEM((width, min(Q_BACK, tokens)), F32),
            pltpu.VMEM((total, 2 * width), F32),
            pltpu.VMEM((n_kv, tokens, 2 * width), BF16),
            pltpu.VMEM((16, tokens), F32),
            pltpu.SemaphoreType.DMA,
        ],
        (low, bands, queries, d_out, out, lse, mark_row, mark_col, cosine, sine, *kv_list),
        20,
        ride,
        before,
    )


def pre_back_kernel(
    n_w,
    n_g,
    n_kv,
    order,
    table,
    x_ref,
    dq_ref,
    cos_ref,
    sin_ref,
    gains_ref,
    dmid_ref,
    ggain_ref,
    att_ref,
    dattn_ref,
    *refs,
):
    dkv_refs, w_refs = refs[:n_kv], refs[n_kv : n_kv + n_w]
    refs = refs[n_kv + n_w :]
    flow_ref, g_refs = refs[0], refs[1 : 1 + n_g]
    w_s, hidt_s, dqkv_s, attt_s, g_s, sem = refs[1 + n_g :]
    tokens, width = x_ref.shape
    start_weights(order, w_refs, w_s, sem)
    gain = gains_ref[0:1, :]
    tile = row_tile(tokens)
    wait_whole(w_s, sem)
    ggain = jnp.zeros((1, width), F32)
    for start in range(0, tokens, tile):
        at = slice(start, start + tile)
        x = x_ref[at, :].astype(F32)
        factor = lax.rsqrt(jnp.mean(x * x, -1, keepdims=True) + EPS)
        normed = x * factor
        hidt_s[:, at] = (normed * gain).T.astype(BF16)
        attt_s[:, at] = att_ref[at, :].astype(F32).T.astype(BF16)
        cosine, sine = cos_ref[at, :], sin_ref[at, :]
        dqkv_s[at, :width] = dq_ref[at, :]
        for col in range(0, 2 * width, 128):
            block = dkv_refs[0][at, col : col + 128].astype(F32)
            for ref in dkv_refs[1:]:
                block = block + ref[at, col : col + 128].astype(F32)
            if col < width:
                block = block * cosine - swap_halves(block) * sine
            dqkv_s[at, width + col : width + col + 128] = block.astype(BF16)
        d_hid = dot_nt(dqkv_s[at, :], w_s[:, : 3 * width])
        ggain = ggain + jnp.sum(d_hid * normed, 0, keepdims=True)
        shaped = d_hid * gain
        flow_ref[at, :] = dmid_ref[at, :] + factor * (
            shaped - normed * jnp.mean(shaped * normed, -1, keepdims=True)
        )
    row = lax.broadcasted_iota(jnp.int32, (128, width), 0)
    both = jnp.where(row == 0, ggain, jnp.where(row == 1, ggain_ref[0:1, :], 0.0))
    g_s[:, 4 * width : 4 * width + 128] = both.T.astype(BF16)
    g_s[:, 4 * width + 128 :] = jnp.zeros((width, 128), BF16)
    g_s[:, 3 * width : 4 * width] = dot(attt_s[...], dattn_ref[...]).astype(BF16)

    def columns(step, carry):
        col = pl.multiple_of(step * 256, 256)
        g_s[:, pl.ds(col, 256)] = dot(hidt_s[...], dqkv_s[:, pl.ds(col, 256)]).astype(BF16)
        return carry

    lax.fori_loop(0, 3 * width // 256, columns, 0)
    send_out(table, g_s, g_refs, sem)
    wait_whole(g_s, sem)


def pre_back(
    order,
    table,
    shapes,
    x,
    dq,
    cosine,
    sine,
    gains,
    d_mid,
    ggain,
    attended,
    d_attn,
    dkv_list,
    weights,
    ride=(),
    before=(),
):
    tokens, width = x.shape
    return call(
        functools.partial(pre_back_kernel, len(weights), len(shapes), len(dkv_list)),
        "pre_back",
        (jax.ShapeDtypeStruct((tokens, width), F32), *shapes),
        [SMEM, SMEM] + [VMEM] * (9 + len(dkv_list)) + [ANY] * len(weights),
        (VMEM, *([ANY] * len(shapes))),
        [
            pltpu.VMEM((width, qkv_cols(width)), BF16),
            pltpu.VMEM((width, tokens), BF16),
            pltpu.VMEM((tokens, 3 * width), BF16),
            pltpu.VMEM((width, tokens), BF16),
            pltpu.VMEM((width, width + qkv_cols(width)), BF16),
            pltpu.SemaphoreType.DMA,
        ],
        (
            order,
            table,
            x,
            dq,
            cosine,
            sine,
            gains,
            d_mid,
            ggain,
            attended,
            d_attn,
            *dkv_list,
            *weights,
        ),
        15,
        ride,
        before,
    )


class Layout:
    def __init__(self, n_rows, n_seq, width, ff):
        self.n_rows, self.n_seq = n_rows, n_seq
        self.paired = n_rows % 2 == 0 and n_seq % 2 == 0
        self.ringed = (
            n_rows % 4 == 0 and (width // n_rows) % 16 == 0 and (ff // n_rows) % 16 == 0
        )

    def device(self, row, seq):
        return row * self.n_seq + seq

    def pairs(self, move):
        return [
            (self.device(row, seq), self.device(*move(row, seq)))
            for row in range(self.n_rows)
            for seq in range(self.n_seq)
        ]

    def send(self, value, move):
        return lax.ppermute(value, BOTH, self.pairs(move))

    def to_core(self, value):
        return self.send(value, lambda row, seq: (row ^ 1, seq))

    def to_y(self, value):
        return self.send(value, lambda row, seq: (row ^ 2, seq))

    def to_z(self, value, hops):
        return self.send(value, lambda row, seq: ((row + 4 * hops) % self.n_rows, seq))

    def to_x(self, value):
        return self.send(value, lambda row, seq: (row, (seq + 1) % self.n_seq))

    def regroup(self, row, seq):
        if not self.paired:
            return (row, seq)
        return (row - row % 2 + seq % 2, (row % 2) * (self.n_seq // 2) + seq // 2)

    def into_groups(self, value):
        return self.send(value, self.regroup) if self.paired else value

    def out_of_groups(self, value):
        if not self.paired:
            return value
        back = [(there, here) for here, there in self.pairs(self.regroup)]
        return lax.ppermute(value, BOTH, back)

    def band(self, row, seq):
        if not self.paired:
            return seq
        return (seq % (self.n_seq // 2)) * 2 + row % 2

    def groups(self):
        places = {}
        for row in range(self.n_rows):
            for seq in range(self.n_seq):
                there = self.regroup(row, seq)
                places.setdefault(row, {})[seq] = self.device(*there)
        return [[places[row][seq] for seq in range(self.n_seq)] for row in range(self.n_rows)]


def on_device(n_rows, n_seq, *args):
    inputs, seg_start, w_q, w_k, w_v, w_o, w_g, w_u, w_d, norm_attn, norm_mlp, cotangent = args
    _, tokens, width = inputs.shape
    ff = w_g.shape[2]
    total = tokens * n_seq
    lay = Layout(n_rows, n_seq, width, ff)
    row_at, seq_at = lax.axis_index("rows"), lax.axis_index("seq")
    ringed = lay.ringed and n_seq == 2
    depth = n_rows // 4

    def bundles(layer):
        gains = jnp.stack([norm_attn[layer], norm_mlp[layer]], 1)
        gains = jnp.pad(gains, ((0, 0), (0, 254)))
        return [
            jnp.concatenate([w_q[layer], w_k[layer], w_v[layer], gains], 1),
            jnp.concatenate([w_o[layer], w_g[layer], w_u[layer]], 1),
            w_d[layer],
        ]

    def split(cols, parts):
        if not ringed:
            return [(0, cols, "offload")]
        found, first = [], 0
        for count, (share, mode) in enumerate(parts, 1):
            size = cols - first if count == len(parts) else round(cols * share / 256) * 256
            found.append((first, size, mode))
            first += size
        return found

    def table(sign, pieces):
        numbers, columns = [], []
        for first, size, mode in pieces:
            if mode == "offload":
                numbers.append(jnp.int32(0))
                columns.append(jnp.int32(first // 128))
                continue
            for core in (0, 1):
                for half in (0, 1) if mode == "half" else (0,):
                    for side in (0, 2):
                        for hop in range(depth):
                            numbers.append(((row_at + sign * 4 * hop) % n_rows) ^ core ^ side)
                            columns.append(
                                first // 128 + (seq_at ^ half) * (size // 256)
                                if mode == "half"
                                else jnp.int32(first // 128)
                            )
        return jnp.stack([jnp.stack(numbers), jnp.stack(columns)]).astype(jnp.int32)

    def shapes(rows, pieces):
        found = []
        for _, size, mode in pieces:
            if mode == "offload":
                found.append(jax.ShapeDtypeStruct((1, rows, size), BF16))
            elif mode == "half":
                found += [jax.ShapeDtypeStruct((2 * depth, rows // n_rows, size // 2), BF16)] * 4
            else:
                found += [jax.ShapeDtypeStruct((depth, rows // n_rows, size), BF16)] * 4
        return found

    def up(value):
        return value.astype(F32)

    class Gather:
        def __init__(self, shard, mode):
            self.mode, self.stacks, self.level = mode, None, 0
            if mode == "offload":
                self.stacks = [lax.all_gather(shard, "rows", axis=0, tiled=True)[None]]
                return
            if mode == "half":
                columns = shard.shape[1] // 2
                shard = lax.dynamic_slice_in_dim(shard, seq_at * columns, columns, 1)
            self.stay, self.flying = [shard], []
            while len(self.flying) + 1 < depth:
                self.flying.append(lay.to_z((self.stay + self.flying)[-1], 1))

        def step(self):
            self.level += 1
            if self.stacks is not None:
                return
            if self.level == 1:
                near = jnp.stack(self.stay + self.flying)
                self.stay, self.flying = [near], [lay.to_y(near)]
            elif self.level == 2 and self.mode == "whole":
                near, far = self.stay[0], self.flying[0]
                self.stacks = [near, far, lay.to_core(near), lay.to_core(far)]
            elif self.level == 2:
                both = jnp.concatenate([self.stay[0], self.flying[0]])
                self.stay, self.flying = [both], [lay.to_x(both)]
            else:
                both, other = self.stay[0], self.flying[0]
                self.stacks = [both, other, lay.to_core(both), lay.to_core(other)]

        def finish(self):
            while self.stacks is None:
                self.step()
            return self.stacks

    class Scatter:
        def __init__(self, stack, mode):
            self.mode, self.sum, self.level, self.old = mode, None, 0, False
            if mode == "offload":
                summed = lax.psum_scatter(stack[0][0], "rows", scatter_dimension=0, tiled=True)
                if n_seq == 2:
                    self.stay, self.flying, self.level = [summed], [lay.to_x(summed)], 9
                else:
                    self.sum = up(lax.psum(summed, "seq"))
                return
            self.flying = [lay.to_core(stack[3]), lay.to_core(stack[2])]
            self.stay = [stack[1], stack[0]]

        def along_z(self, both):
            sent = [both[hop].astype(BF16) for hop in range(1, depth)]
            self.flying = [lay.to_z(value, hop) for hop, value in enumerate(sent, 1)]
            self.stay = [both[0]]
            return sent

        def step(self):
            if self.sum is not None:
                return []
            self.level += 1
            half = self.mode == "half"
            stay, flying = self.stay, self.flying
            if self.level == 1:
                first = (up(stay[0]) + up(flying[0])).astype(BF16)
                self.stay = [stay[1]]
                self.flying = [lay.to_x(first) if half else lay.to_y(first), flying[1]]
                return [first]
            if self.level == 2:
                both = up(stay[0]) + up(flying[1]) + up(flying[0])
                if not half:
                    return self.along_z(both)
                far = both[depth:].astype(BF16)
                self.stay, self.flying = [both[:depth]], [lay.to_y(far)]
                return [far]
            if self.level == 3 and half:
                return self.along_z(stay[0] + up(flying[0]))
            if self.level == (4 if half else 3):
                total = up(stay[0])
                for value in flying:
                    total = total + up(value)
                total = total.astype(BF16)
                self.stay, self.flying = [total], [lay.to_x(total)]
                return [total]
            mine, other = stay[0], flying[0]
            if not half:
                self.sum = up(mine) + up(other)
                return []
            self.sum = up(
                jnp.where(
                    seq_at == 0,
                    jnp.concatenate([mine, other], 1),
                    jnp.concatenate([other, mine], 1),
                )
            )
            return []

        def finish(self):
            while self.sum is None:
                self.step()
            return self.sum

    def scatters(arrays, pieces):
        found, at = [], 0
        for _, _, mode in pieces:
            size = 1 if mode == "offload" else 4
            found.append(Scatter(arrays[at : at + size], mode))
            at += size
        return found

    def joined(chains):
        sums = [chain.finish() for chain in chains]
        return sums[0] if len(sums) == 1 else jnp.concatenate(sums, 1)

    x_in = lay.into_groups(inputs[0])
    starts_mine = lay.into_groups(seg_start[0])
    d_top = lay.into_groups(cotangent[0])
    groups = lay.groups()
    half_seq = n_seq // 2
    band = (seq_at % half_seq) * 2 + row_at % 2 if lay.paired else seq_at
    two = lay.paired and n_seq == 2

    def exchange(value):
        if two:
            return [value, lay.to_core(value)]
        whole = lax.all_gather(value, BOTH, axis=0, axis_index_groups=groups)
        return [whole[index] for index in range(n_seq)]

    if two:
        bands = jnp.stack([band, band, 1 - band]).astype(jnp.int32)
    else:
        bands = jnp.concatenate([band[None], jnp.arange(n_seq)]).astype(jnp.int32)

    index = band * tokens + jnp.arange(tokens, dtype=jnp.int32)
    positions = jnp.where(starts_mine >= 0, index - starts_mine, 0)
    inverse = THETA ** (-jnp.arange(HEAD_DIM // 2, dtype=F32) * 2.0 / HEAD_DIM)
    angles = positions.astype(F32)[:, None] * inverse
    cosine = jnp.tile(jnp.cos(angles), (1, 4))
    sine = jnp.sin(angles)
    sine = jnp.concatenate([-sine, sine, -sine, sine], 1)
    marks = jnp.where(starts_mine >= 0, starts_mine, -1 - index)
    mark_row = jnp.broadcast_to(marks[None, :], (8, tokens))
    pieces = exchange(marks)
    if two:
        marks_all = jnp.where(
            band == 0, jnp.concatenate(pieces), jnp.concatenate([pieces[1], pieces[0]])
        )
    else:
        marks_all = jnp.concatenate(pieces)
    mark_col = jnp.broadcast_to(marks_all[:, None], (total, 128))
    reach = jnp.where(starts_mine >= 0, starts_mine, index)
    low = jnp.min(reach.reshape(-1, Q_TILE), 1).astype(jnp.int32)

    in_widths = (qkv_cols(width), width + 2 * ff, width)
    out_widths = (width + qkv_cols(width), 2 * ff, width)
    in_pieces = [[split(c, p) for c, p in zip(in_widths, parts)] for parts in IN_PARTS]
    out_pieces = [[split(c, p) for c, p in zip(out_widths, parts)] for parts in OUT_PARTS]
    known = {}

    def table_of(sign, pieces):
        key = (sign, *pieces)
        if key not in known:
            known[key] = table(sign, pieces)
        return known[key]

    orders = [[table_of(-1, pieces) for pieces in in_pieces[layer]] for layer in range(LAYERS)]
    tables = [[table_of(1, pieces) for pieces in out_pieces[layer]] for layer in range(LAYERS)]

    def gathers(shard, pieces):
        return [Gather(shard[:, first : first + size], mode) for first, size, mode in pieces]

    def arrived(chains):
        return [stack for chain in chains for stack in chain.finish()]

    kept = []
    current = x_in
    weights = []

    def near_of(bundles_of_chains):
        found = []
        for chains_here in bundles_of_chains:
            for chain in chains_here:
                if chain.stacks is None:
                    chain.step()
                    found += chain.stay
        return found

    shards = bundles(0)
    moving = [[gathers(shards[0], in_pieces[0][0])], None]
    if ringed:
        _ = ([value for chain in moving[0][0] for value in chain.flying], shards[1:])
    moving[0] += [gathers(s, p) for s, p in zip(shards[1:], in_pieces[0][1:])]
    for layer in range(LAYERS):
        last = layer + 1 == LAYERS
        o_qkv, o_ogu, o_down = orders[layer]
        w_qkv = arrived(moving[layer][0])
        (queries, kv, gains), ridden = pre(
            o_qkv,
            current,
            cosine,
            sine,
            w_qkv,
            ride=[] if last else bundles(layer + 1),
        )
        kv_list = exchange(kv)
        (attended, lse), _ = attend(
            low,
            bands,
            queries,
            mark_row,
            mark_col,
            kv_list,
            total,
        )
        before = []
        if not last:
            moving[layer + 1] = [gathers(s, p) for s, p in zip(ridden, in_pieces[layer + 1])]
        w_ogu, w_down = arrived(moving[layer][1]), arrived(moving[layer][2])
        (result, mid, gu), _ = post(
            o_ogu, o_down, ff, current, attended, gains, w_ogu, w_down, before=before
        )
        kept.append((current, queries, kv_list, attended, lse, mid, gu, gains))
        weights.append((w_qkv, w_ogu, w_down))
        current = result
    output = lay.out_of_groups(current.astype(BF16)).astype(F32)

    flow = d_top
    chains = [None] * LAYERS
    live = []

    def through(kernel, *args, still=(), **more):
        if not ringed:
            return kernel(*args, **more)[0]
        sent = more.pop("before", [])
        for chain in live:
            if chain.level < 9 and chain not in still:
                sent = sent + (chain.step() if chain.old else [])
            chain.old = True
        holders = [chain for chain in live if chain.sum is None and chain.level < 9]
        ride = [value for chain in holders for value in chain.stay]
        results, ridden = kernel(*args, ride=ride, before=sent, **more)
        for chain in holders:
            chain.stay, ridden = ridden[: len(chain.stay)], ridden[len(chain.stay) :]
        return results

    for layer in reversed(range(LAYERS)):
        x, queries, kv_list, attended, lse, mid, gu, gains = kept[layer]
        o_qkv, o_ogu, o_down = orders[layer]
        w_qkv, w_ogu, w_down = weights[layer]
        t_qkv, t_gu, t_down = tables[layer]
        p_qkv, p_gu, p_down = out_pieces[layer]
        s_gu, s_down = shapes(width, p_gu), shapes(ff, p_down)
        results = through(
            mlp_back, o_down, (t_gu, t_down), (s_gu, s_down), flow, mid, gu, gains, w_down
        )
        dgu = results[0]
        c_gu = scatters(results[1 : 1 + len(s_gu)], p_gu)
        c_down = scatters(results[1 + len(s_gu) :], p_down)
        live += c_gu + c_down
        d_mid, d_attn, d_att, ggain = through(mid_back, o_ogu, flow, mid, dgu, gains, w_ogu)
        results = through(
            attend_back,
            low,
            bands,
            queries,
            d_att,
            attended,
            lse,
            mark_row,
            mark_col,
            cosine,
            sine,
            kv_list,
            total,
        )
        dq, dkv = results[0], results[1:]
        if two:
            dkv_list = [dkv[0], lay.to_core(dkv[1])]
        else:
            dkv_list = [
                lax.psum_scatter(
                    jnp.stack(dkv), BOTH, scatter_dimension=0, axis_index_groups=groups
                )
            ]
        s_qkv = shapes(width, p_qkv)
        results = through(
            pre_back,
            o_qkv,
            t_qkv,
            s_qkv,
            x,
            dq,
            cosine,
            sine,
            gains,
            d_mid,
            ggain,
            attended,
            d_attn,
            dkv_list,
            w_qkv,
            before=[output] if layer == 0 else [],
            still=live if layer > 0 else [],
        )
        flow = results[0]
        c_qkv = scatters(results[1:], p_qkv)
        live += c_qkv
        chains[layer] = (c_qkv, c_gu, c_down)
    laps = 0
    while ringed and any(chain.sum is None and chain.level < 9 for chain in live):
        done = [
            value
            for layer, lap in ((1, 0), (0, 2))
            for chain in chains[layer][1]
            if chain.level == 9 and lap == laps
            for value in chain.flying
        ]
        through(lambda ride, before: ([], gate(before, ride)), before=done)
        laps += 1
    grads = [[joined(part) for part in chains[layer]] for layer in range(LAYERS)]
    grad_input = lay.out_of_groups(flow.astype(BF16)).astype(F32)

    def stack(which, first, size):
        return jnp.stack([grads[layer][which][:, first : first + size] for layer in range(LAYERS)])

    return (
        output[None],
        grad_input[None],
        stack(0, 0, width),
        stack(0, width, width),
        stack(0, 2 * width, width),
        stack(0, 3 * width, width),
        stack(1, 0, ff),
        stack(1, ff, ff),
        stack(2, 0, width),
        stack(0, 4 * width, 1)[..., 0],
        stack(0, 4 * width + 1, 1)[..., 0],
    )


def solution(mesh):
    rows3, rows2 = P("rows", "seq", None), P("rows", "seq")
    weight, vector = P(None, "rows", None), P(None, "rows")
    return jax.shard_map(
        functools.partial(on_device, mesh.shape["rows"], mesh.shape["seq"]),
        mesh=mesh,
        in_specs=(rows3, rows2, *([weight] * 7), vector, vector, rows3),
        out_specs=(rows3, rows3, *([weight] * 7), vector, vector),
        check_vma=False,
    )
```
